32 devices in a mesh: dp: 2 (over x), expert: 4 (over z), tensor: 4 (over y, core).
Axes of the slice: x: 2, y: 2, z: 4, core: 2. Of those that a mesh axis runs over, the one named last changes fastest.
Arguments:
- tokens: bfloat16 [192, 3072], P(('dp', 'expert', 'tensor')), parts along dimension 0, may hold values from -200 to 200
- norm_gain: float32 [3072], replicated, may hold values from 0.1 to 1.9
- router: bfloat16 [3072, 4], replicated, may hold values from -0.109375 to 0.109375
- up_weight: bfloat16 [4, 3072, 16384], P('expert', None, 'tensor'), may hold values from -0.109375 to 0.109375
- down_weight: bfloat16 [4, 3072, 16384], P('expert', None, 'tensor'), may hold values from -0.046875 to 0.046875
- expert_ids: int32 [192, 2], P(('dp', 'expert', 'tensor')), parts along dimension 0, may hold values from 0 to 3, as said below
- bin_slots: int32 [192, 2], P(('dp', 'expert', 'tensor')), parts along dimension 0, may hold values from 0 to 14, as said below
- kept_mask: int32 [192, 2], P(('dp', 'expert', 'tensor')), parts along dimension 0, may hold values from 0 to 1, as said below
- grad_out: bfloat16 [192, 3072], P(('dp', 'expert', 'tensor')), parts along dimension 0, may hold values from -6 to 6
Outputs:
- mixed: bfloat16 [192, 3072], P(('dp', 'expert', 'tensor')), parts along dimension 0
- grad_tokens: bfloat16 [192, 3072], P(('dp', 'expert', 'tensor')), parts along dimension 0
The draws below stay inside these ranges and needn't reach their ends.
There are 2 independent parts, one for each index of `dp`. The reference program is written for one: setup_inputs(seed, part) draws one part's arguments, and reference() takes and returns one part's arrays. A program takes and returns all parts, laid end to end along the dimension named above; an argument that names none is the same for every part. Nothing has to cross between parts.
Inputs may be any that keep to these rules, and one draw needn't show every extreme that they name: `expert_ids`: each token names 2 different experts. `bin_slots`: in each group the choices are taken in order of token, first choice before second; a choice is kept while its expert has fewer than 15 kept choices of the group and then holds the number of kept choices of that group and expert before it; a dropped choice holds 0. In every group some expert receives 15 kept choices. `kept_mask`: follows the rule stated for bin_slots.
All inputs are finite; a program needn't handle non-finite values.
Results may differ from the reference program's by a relative error of at most 0.0069.
Values may be sent and summed in bfloat16 or wider, within the bound.
No kernel may reach another device: no remote copies, remote signals or barrier semaphores. Data moves between devices by JAX's collectives and lax.ppermute only.
A program may use at most 128 MiB of HBM per device.

```python
import jax
import jax.numpy as jnp
from jax import lax

D = 3072
FF = 16384
TOP = 2
TOK_DEV = 6
EXPERT_TOTAL = 4
GROUPS = 4
TOKENS = 96
GCAP = 15
BIN = 60


def route_plan(key):
    keys = jax.random.split(key, 4)
    baseline_score = jax.random.randint(keys[0], (TOKENS, EXPERT_TOTAL), 0, 65536)
    preferred_bias = jax.random.randint(keys[1], (EXPERT_TOTAL,), 0, 32768)
    favoured_expert = jax.random.randint(keys[2], (GROUPS,), 0, EXPERT_TOTAL)
    sources = TOKENS // (TOK_DEV * GROUPS)
    ranking = jax.vmap(lambda subkey: jax.random.permutation(subkey, sources))(jax.random.split(keys[3], GROUPS))
    position = jnp.arange(TOKENS, dtype=jnp.int32)
    group_lookup = position // TOK_DEV % GROUPS
    source_of = position // (TOK_DEV * GROUPS)
    forced_choice = ranking[group_lookup, source_of] < 3
    column_labels = jnp.arange(EXPERT_TOTAL, dtype=jnp.int32)
    extra_boost = jnp.where(forced_choice[:, None] & (column_labels[None, :] == favoured_expert[group_lookup][:, None]), 262144, 0)
    router_scores = (baseline_score + preferred_bias[None, :] + extra_boost) * EXPERT_TOTAL + column_labels[None, :]
    expert_ids = lax.top_k(router_scores, TOP)[1].astype(jnp.int32)
    matches = (expert_ids[:, :, None] == column_labels[None, None, :]).astype(jnp.int32)
    ordered = matches.reshape(sources, GROUPS, TOK_DEV * TOP, EXPERT_TOTAL).transpose(1, 0, 2, 3).reshape(GROUPS, sources * TOK_DEV * TOP, EXPERT_TOTAL)
    before = jnp.cumsum(ordered, axis=1) - ordered
    arrival = before.reshape(GROUPS, sources, TOK_DEV * TOP, EXPERT_TOTAL).transpose(1, 0, 2, 3).reshape(TOKENS, TOP, EXPERT_TOTAL)
    arrival_slot = jnp.sum(arrival * matches, axis=2).astype(jnp.int32)
    kept_mask = (arrival_slot < GCAP).astype(jnp.int32)
    bin_slots = jnp.where(kept_mask == 1, arrival_slot, 0).astype(jnp.int32)
    return (expert_ids, bin_slots, kept_mask)


def draw_expert_ids(key, part):
    plan = route_plan(key)
    return plan[0]


def draw_bin_slots(key, part):
    plan = route_plan(key)
    return plan[1]


def draw_kept_mask(key, part):
    plan = route_plan(key)
    return plan[2]


def draw_tokens(key, part):
    key = jax.random.fold_in(key, 11)
    keys = jax.random.split(key, 1)
    return jnp.clip(jax.random.normal(keys[0], (TOKENS, D)), -6.0, 6.0).astype(jnp.bfloat16)


def steps_of(key, extent, shards, low, top_value):
    gain = 1.0
    for dim, parts in shards:
        heights = jax.random.uniform(jax.random.fold_in(jax.random.fold_in(key, 6), dim), (parts,), jnp.float32, low / len(shards), top_value / len(shards))
        gain = gain * jnp.repeat(jnp.exp(heights), extent[dim] // parts).reshape((-1,) + (1,) * (len(extent) - 1 - dim))
    return gain


def bell_draw(own_key, dims, deviation, most, shards=(), kind=jnp.bfloat16):
    entries = deviation * jax.random.normal(own_key, dims, jnp.float32)
    if shards:
        entries = entries * steps_of(own_key, dims, shards, -0.22, 0.18)
    return jnp.clip(entries, -most, most).astype(kind)


def setup_inputs(seed: int = 0, part: int = 0) -> dict:
    splits = jax.random.split(jax.random.key(seed), 10)
    own_keys = jax.random.split(jax.random.fold_in(splits[9], part), 10)
    return {
        "tokens": draw_tokens(jax.random.fold_in(jax.random.fold_in(splits[9], part), 71), part),
        "norm_gain": jnp.clip(1.0 + 0.18 * jax.random.normal(splits[1], (D,), jnp.float32), 0.1, 1.9),
        "router": bell_draw(splits[2], (D, EXPERT_TOTAL), D ** -0.5, 0.109375),
        "up_weight": bell_draw(splits[3], (EXPERT_TOTAL, D, FF), D ** -0.5, 0.109375, ((0, 4), (2, 4))),
        "down_weight": bell_draw(splits[4], (EXPERT_TOTAL, D, FF), FF ** -0.5, 0.046875, ((0, 4), (2, 4))),
        "expert_ids": draw_expert_ids(jax.random.fold_in(jax.random.fold_in(splits[9], part), 71), part),
        "bin_slots": draw_bin_slots(jax.random.fold_in(jax.random.fold_in(splits[9], part), 71), part),
        "kept_mask": draw_kept_mask(jax.random.fold_in(jax.random.fold_in(splits[9], part), 71), part),
        "grad_out": bell_draw(own_keys[8], (TOKENS, D), 1.0, 6.0, ((0, 16),)),
    }


root_two_pi = 0.7978845608028654
cubic_term = 0.044715

def gelu_tanh(inputs):
    return 0.5 * inputs * (1.0 + jnp.tanh(root_two_pi * (inputs + cubic_term * inputs * inputs * inputs)))

def gelu_slope(inputs):
    inner_tanh = jnp.tanh(root_two_pi * (inputs + cubic_term * inputs * inputs * inputs))
    return 0.5 * (1.0 + inner_tanh) + 0.5 * inputs * (1.0 - inner_tanh * inner_tanh) * root_two_pi * (1.0 + 3.0 * cubic_term * inputs * inputs)

def reference(tokens, norm_gain, router, up_weight, down_weight, expert_ids, bin_slots, kept_mask, grad_out):
    widened = tokens.astype(jnp.float32)
    meansq = lax.optimization_barrier(jnp.mean(widened * widened, axis=1, keepdims=True))
    inverse = lax.rsqrt(meansq + 1e-06)
    normed = (widened * inverse * norm_gain).astype(jnp.bfloat16)
    logits = jnp.dot(normed, router, preferred_element_type=jnp.float32)
    choose = (expert_ids[:, :, None] == jnp.arange(EXPERT_TOTAL, dtype=jnp.int32)[None, None, :]).astype(jnp.float32)
    picked = lax.optimization_barrier(jnp.sum(choose * logits[:, None, :], axis=2))
    first_gate = 1.0 / (1.0 + jnp.exp(picked[:, 1] - picked[:, 0]))
    second_gate = 1.0 / (1.0 + jnp.exp(picked[:, 0] - picked[:, 1]))
    gate_pair = jnp.stack([first_gate, second_gate], axis=1)
    kept_float = kept_mask.astype(jnp.float32)
    group_lookup = jnp.arange(TOKENS, dtype=jnp.int32) // TOK_DEV % GROUPS
    bin_row = group_lookup[:, None] * GCAP + bin_slots
    scaled = ((kept_float * gate_pair)[:, :, None] * grad_out.astype(jnp.float32)[:, None, :]).astype(jnp.bfloat16)
    rows_in = jnp.broadcast_to(normed[:, None, :], (TOKENS, TOP, D)).reshape(TOKENS * TOP, D)
    rows_grad = scaled.reshape(TOKENS * TOP, D)

    def expert_pass(expert):
        belongs = (expert_ids == expert) & (kept_mask == 1)
        row_index = jnp.where(belongs, bin_row, BIN).reshape(-1).astype(jnp.int32)
        bin_in = jnp.zeros((BIN + 1, D), normed.dtype).at[row_index].add(rows_in)[:BIN]
        bin_grad = jnp.zeros((BIN + 1, D), scaled.dtype).at[row_index].add(rows_grad)[:BIN]
        weight_in = up_weight[expert]
        weight_out = down_weight[expert]
        hidden = jnp.dot(bin_in, weight_in, preferred_element_type=jnp.float32)
        active = gelu_tanh(hidden).astype(jnp.bfloat16)
        bin_out = jnp.dot(active, weight_out.T, preferred_element_type=jnp.float32).astype(jnp.bfloat16)
        back_act = jnp.dot(bin_grad, weight_out, preferred_element_type=jnp.float32)
        back_hidden = (back_act * gelu_slope(hidden)).astype(jnp.bfloat16)
        bin_back = jnp.dot(back_hidden, weight_in.T, preferred_element_type=jnp.float32).astype(jnp.bfloat16)
        return (bin_out, bin_back)
    expert_outs, expert_backs = lax.map(expert_pass, jnp.arange(EXPERT_TOTAL, dtype=jnp.int32))
    safe_row = jnp.where(kept_mask == 1, bin_row, 0).astype(jnp.int32)
    keep_rows = (kept_mask == 1)[:, :, None]
    chosen = jnp.where(keep_rows, expert_outs[expert_ids, safe_row], jnp.zeros((), expert_outs.dtype))
    returned = jnp.where(keep_rows, expert_backs[expert_ids, safe_row], jnp.zeros((), expert_backs.dtype))
    chosen_float = chosen.astype(jnp.float32)
    mixed = lax.optimization_barrier(jnp.sum(gate_pair[:, :, None] * chosen_float, axis=1)).astype(jnp.bfloat16)
    gate_grad = lax.optimization_barrier(jnp.sum(grad_out.astype(jnp.float32)[:, None, :] * chosen_float, axis=2))
    spread = gate_pair[:, 0] * gate_pair[:, 1] * (gate_grad[:, 0] - gate_grad[:, 1])
    logit_grad = jnp.stack([spread, -spread], axis=1)
    router_grad = lax.optimization_barrier(jnp.sum(logit_grad[:, :, None] * choose, axis=1))
    normed_grad = lax.optimization_barrier(jnp.sum(returned.astype(jnp.float32), axis=1)) + jnp.dot(router_grad, router.astype(jnp.float32).T, precision=lax.Precision.HIGHEST)
    upstream = normed_grad * norm_gain
    grad_tokens = inverse * (upstream - widened * inverse * inverse * lax.optimization_barrier(jnp.mean(upstream * widened, axis=1, keepdims=True)))
    return (mixed, grad_tokens.astype(jnp.bfloat16))
```

```python
import functools

import jax
import jax.numpy as jnp
from jax import lax
from jax.experimental import pallas as pl
from jax.experimental.pallas import tpu as pltpu
from jax.sharding import PartitionSpec as P

GCAP = 15
SLOTS = 16
PAD = 8
LANES = 128
CHUNK = 512

root_two_pi = 0.7978845608028654
cubic_term = 0.044715

VM = pl.BlockSpec(memory_space=pltpu.VMEM)
SM = pl.BlockSpec(memory_space=pltpu.SMEM)


def gelu_both(v):
    t = jnp.tanh(root_two_pi * (v + cubic_term * v * v * v))
    value = 0.5 * v * (1.0 + t)
    slope = 0.5 * (1.0 + t) + 0.5 * v * (1.0 - t * t) * root_two_pi * (
        1.0 + 3.0 * cubic_term * v * v
    )
    return value, slope


def column(ref, choice, rows):
    row = lax.broadcasted_iota(jnp.int32, (rows, LANES), 0)
    out = jnp.zeros((rows, LANES), jnp.int32)
    for r in range(rows):
        out = jnp.where(row == r, ref[choice, r], out)
    return out


def pack_kernel(ids, slots, kept, tok, grad, gain, router, *outs):
    messages, gates_ref = outs[:-1], outs[-1]
    rows, width = tok.shape
    experts = router.shape[0]
    me = lax.axis_index("expert")
    x = tok[...].astype(jnp.float32)
    g = grad[...].astype(jnp.float32)
    inverse = lax.rsqrt(jnp.mean(x * x, axis=1, keepdims=True) + 1e-06)
    normed = (x * inverse * gain[...]).astype(jnp.bfloat16)
    wide = normed.astype(jnp.float32)
    id0, id1 = column(ids, 0, rows), column(ids, 1, rows)
    slot0, slot1 = column(slots, 0, rows), column(slots, 1, rows)
    kept0, kept1 = column(kept, 0, rows), column(kept, 1, rows)
    pick0 = jnp.zeros((rows, LANES), jnp.float32)
    pick1 = jnp.zeros((rows, LANES), jnp.float32)
    for e in range(experts):
        logit = jnp.sum(wide * router[e : e + 1, :].astype(jnp.float32), axis=1, keepdims=True)
        pick0 = jnp.where(id0 == e, logit, pick0)
        pick1 = jnp.where(id1 == e, logit, pick1)
    gate0 = 1.0 / (1.0 + jnp.exp(pick1 - pick0))
    gate1 = 1.0 / (1.0 + jnp.exp(pick0 - pick1))
    gates_ref[0, ...] = gate0
    gates_ref[1, ...] = gate1
    for k, out in enumerate(messages):
        expert = me ^ k
        take0 = (id0 == expert) & (kept0 == 1)
        take1 = (id1 == expert) & (kept1 == 1)
        gate = jnp.where(take0, gate0, jnp.where(take1, gate1, 0.0))
        slot = jnp.where(take0, slot0, jnp.where(take1, slot1, -1))
        out[:, : 2 * width] = jnp.zeros((PAD, 2 * width), jnp.bfloat16)
        out[:, 2 * width :] = jnp.full((PAD, LANES), -1.0, jnp.bfloat16)
        out[0:rows, :width] = normed
        out[0:rows, width : 2 * width] = (gate[:, 0:1] * g).astype(jnp.bfloat16)
        out[0:rows, 2 * width :] = slot.astype(jnp.float32).astype(jnp.bfloat16)


def bin_kernel(width, *refs):
    messages, (bins, placed_ref) = refs[:-2], refs[-2:]
    rows = jnp.concatenate([m[...].astype(jnp.float32) for m in messages], axis=0)
    lane = lax.broadcasted_iota(jnp.int32, (rows.shape[0], LANES), 1).astype(jnp.float32)
    placed = jnp.where(rows[:, 2 * width :] == lane, 1.0, 0.0)
    placed_ref[...] = placed
    onehot = placed.T[:SLOTS].astype(jnp.bfloat16)
    packed = rows[:, : 2 * width].astype(jnp.bfloat16)
    filled = jnp.dot(onehot, packed, preferred_element_type=jnp.float32).astype(jnp.bfloat16)
    bins[0:SLOTS, :] = filled[:, :width]
    bins[SLOTS : 2 * SLOTS, :] = filled[:, width:]


def expert_kernel(groups, *refs):
    bins = refs[:groups]
    up, down, keep, send, x, g, acc_out, acc_back = refs[groups:]
    step = pl.program_id(0)
    rows = groups * SLOTS

    @pl.when(step == 0)
    def _():
        x[...] = jnp.zeros_like(x)
        g[...] = jnp.zeros_like(g)
        for j in range(groups):
            x[j * SLOTS : (j + 1) * SLOTS, :] = bins[j][0:SLOTS, :]
            g[j * SLOTS : (j + 1) * SLOTS, :] = bins[j][SLOTS : 2 * SLOTS, :]
        acc_out[...] = jnp.zeros_like(acc_out)
        acc_back[...] = jnp.zeros_like(acc_back)

    w_in, w_out = up[0], down[0]
    hidden = jnp.dot(x[...], w_in, preferred_element_type=jnp.float32)[:rows]
    back_act = jnp.dot(g[...], w_out, preferred_element_type=jnp.float32)[:rows]
    value, slope = gelu_both(hidden)
    active = value.astype(jnp.bfloat16)
    back_hidden = (back_act * slope).astype(jnp.bfloat16)
    over = (((1,), (1,)), ((), ()))
    acc_out[...] += lax.dot_general(w_out, active, over, preferred_element_type=jnp.float32)
    acc_back[...] += lax.dot_general(w_in, back_hidden, over, preferred_element_type=jnp.float32)

    @pl.when(step == pl.num_programs(0) - 1)
    def _():
        width = x.shape[1]
        for c in range(0, width, 512):
            for half, acc in ((0, acc_out), (1, acc_back)):
                part = acc[c : c + 512, :].T.astype(jnp.bfloat16)
                for j in range(groups):
                    to = send if j % 2 else keep
                    at = (j // 2) * 2 * SLOTS + half * SLOTS
                    to[at : at + SLOTS, c : c + 512] = part[j * SLOTS : (j + 1) * SLOTS]


def sum_reply_kernel(n_parts, *refs):
    parts, placed, replies = refs[:n_parts], refs[n_parts], refs[n_parts + 1 :]
    width = parts[0].shape[1]
    total = parts[0][0 : 2 * SLOTS, :].astype(jnp.float32)
    for p in parts[1:]:
        total = total + p[0 : 2 * SLOTS, :].astype(jnp.float32)
    total = total.astype(jnp.bfloat16)
    onehot = placed[...][:, :SLOTS].astype(jnp.bfloat16)
    for half in (0, 1):
        rows = total[half * SLOTS : (half + 1) * SLOTS, :]
        spread = jnp.dot(onehot, rows, preferred_element_type=jnp.float32)
        for k, out in enumerate(replies):
            out[:, half * width : (half + 1) * width] = spread[k * PAD : (k + 1) * PAD].astype(
                jnp.bfloat16
            )


def finish_kernel(ids, tok, grad, gain, router, gates, *refs):
    replies, (mixed, grad_tokens) = refs[:-2], refs[-2:]
    rows, width = tok.shape
    experts = router.shape[0]
    me = lax.axis_index("expert")
    x = tok[...].astype(jnp.float32)
    g = grad[...].astype(jnp.float32)
    inverse = lax.rsqrt(jnp.mean(x * x, axis=1, keepdims=True) + 1e-06)
    id0, id1 = column(ids, 0, rows), column(ids, 1, rows)
    gate0, gate1 = gates[0][:, 0:1], gates[1][:, 0:1]
    chosen0 = jnp.zeros((rows, width), jnp.float32)
    chosen1 = jnp.zeros((rows, width), jnp.float32)
    back = jnp.zeros((rows, width), jnp.float32)
    for k, reply in enumerate(replies):
        expert = me ^ k
        row = reply[0:rows, :].astype(jnp.float32)
        chosen0 = jnp.where(id0[:, 0:1] == expert, row[:, :width], chosen0)
        chosen1 = jnp.where(id1[:, 0:1] == expert, row[:, :width], chosen1)
        back = back + row[:, width:]
    mixed[...] = (gate0 * chosen0 + gate1 * chosen1).astype(jnp.bfloat16)
    grad0 = jnp.sum(g * chosen0, axis=1, keepdims=True)
    grad1 = jnp.sum(g * chosen1, axis=1, keepdims=True)
    spread = gate0 * gate1 * (grad0 - grad1)
    for e in range(experts):
        line = router[e : e + 1, :].astype(jnp.float32)
        weight = jnp.where(id0[:, 0:1] == e, spread, 0.0) - jnp.where(
            id1[:, 0:1] == e, spread, 0.0
        )
        back = back + weight * line
    upstream = back * gain[...]
    mean = jnp.mean(upstream * x, axis=1, keepdims=True)
    grad_tokens[...] = (inverse * (upstream - x * inverse * inverse * mean)).astype(jnp.bfloat16)


def call(body, out_shape, in_specs, args, **kwargs):
    out_specs = jax.tree.map(lambda _: VM, out_shape)
    return pl.pallas_call(
        body, out_shape=out_shape, in_specs=in_specs, out_specs=out_specs, **kwargs
    )(*args)


def shards(
    tokens, norm_gain, router, up_weight, down_weight, expert_ids, bin_slots, kept_mask, grad_out
):
    rows, width = tokens.shape
    hidden = up_weight.shape[2]
    experts = lax.axis_size("expert")
    groups = lax.axis_size("tensor")
    bf16, f32 = jnp.bfloat16, jnp.float32

    def swap(array, axis, mask):
        n = lax.axis_size(axis)
        return lax.ppermute(array, axis, [(i, i ^ mask) for i in range(n)])

    ids, slots, kept = expert_ids.T, bin_slots.T, kept_mask.T
    gain, lines = norm_gain.reshape(1, width), router.T

    message = jax.ShapeDtypeStruct((PAD, 2 * width + LANES), bf16)
    *messages, gates = call(
        pack_kernel,
        [message] * experts + [jax.ShapeDtypeStruct((2, rows, LANES), f32)],
        [SM] * 3 + [VM] * 4,
        (ids, slots, kept, tokens, grad_out, gain, lines),
    )
    arrived = [messages[0]] + [swap(messages[k], "expert", k) for k in range(1, experts)]

    own, placed = call(
        functools.partial(bin_kernel, width),
        [
            jax.ShapeDtypeStruct((2 * SLOTS, width), bf16),
            jax.ShapeDtypeStruct((experts * PAD, LANES), f32),
        ],
        [VM] * experts,
        arrived,
    )

    bins = {0: own}
    mask = groups // 2
    while mask:
        bins.update({j | mask: swap(b, "tensor", mask) for j, b in bins.items()})
        mask //= 2

    tall = max(groups * SLOTS, 128)
    chunk = min(CHUNK, hidden)
    half = jax.ShapeDtypeStruct((groups * SLOTS, width), bf16)
    whole = pl.BlockSpec((2 * SLOTS, width), lambda i: (0, 0))
    weight = pl.BlockSpec((1, width, chunk), lambda i: (0, 0, i))
    keep, send = pl.pallas_call(
        functools.partial(expert_kernel, groups),
        out_shape=[half, half],
        grid=(hidden // chunk,),
        in_specs=[whole] * groups + [weight] * 2,
        out_specs=[pl.BlockSpec(half.shape, lambda i: (0, 0))] * 2,
        scratch_shapes=[
            pltpu.VMEM((tall, width), bf16),
            pltpu.VMEM((tall, width), bf16),
            pltpu.VMEM((width, groups * SLOTS), f32),
            pltpu.VMEM((width, groups * SLOTS), f32),
        ],
        compiler_params=pltpu.CompilerParams(vmem_limit_bytes=48 * 2**20),
    )(*[bins[j] for j in range(groups)], up_weight, down_weight)

    got = swap(send, "tensor", 1)
    mask = 2
    left = {2 * i: slice(2 * SLOTS * i, 2 * SLOTS * (i + 1)) for i in range(groups // 2)}
    sums = {
        j: (keep[s].astype(f32) + got[s].astype(f32)) for j, s in left.items() if j
    }
    firsts = [keep, got]
    while mask < groups:
        going = {j: sums[j].astype(bf16) for j in sums if j & mask}
        came = {j ^ mask: swap(a, "tensor", mask) for j, a in going.items()}
        for j, a in came.items():
            if j == 0:
                firsts.append(a)
            else:
                sums[j] = sums[j] + a.astype(f32)
        sums = {j: a for j, a in sums.items() if not j & mask}
        mask *= 2

    replies = call(
        functools.partial(sum_reply_kernel, len(firsts)),
        [jax.ShapeDtypeStruct((PAD, 2 * width), bf16)] * experts,
        [VM] * (len(firsts) + 1),
        (*firsts, placed),
    )
    answers = [replies[0]] + [swap(replies[k], "expert", k) for k in range(1, experts)]

    result = jax.ShapeDtypeStruct((rows, width), bf16)
    mixed, grad_tokens = call(
        finish_kernel,
        [result, result],
        [SM] + [VM] * (5 + experts),
        (ids, tokens, grad_out, gain, lines, gates, *answers),
    )
    return mixed, grad_tokens


def solution(mesh):
    split = P(("dp", "expert", "tensor"), None)
    weights = P("expert", None, "tensor")
    return jax.shard_map(
        shards,
        mesh=mesh,
        in_specs=(split, P(), P(), weights, weights, split, split, split, split),
        out_specs=(split, split),
        check_vma=False,
    )
```

```python
import functools

import jax
import jax.numpy as jnp
from jax import lax
from jax.experimental import pallas as pl
from jax.experimental.pallas import tpu as pltpu
from jax.sharding import PartitionSpec as P

GCAP = 15
SLOTS = 16
PAD = 8
LANES = 128
STEP = 512
SMALL = 4 * 2**20
FIELD = 32

root_two_pi = 0.7978845608028654
cubic_term = 0.044715

VM = pl.BlockSpec(memory_space=pltpu.VMEM)
SM = pl.BlockSpec(memory_space=pltpu.SMEM)
FAR = pl.BlockSpec(memory_space=pltpu.HBM)


def layout(rows, width):
    spare = PAD - rows
    pieces = -(-rows // spare)
    tail = 2 * width // (pieces + 1)
    return pieces, tail, 2 * width - tail


def gelu_both(v):
    t = jnp.tanh(root_two_pi * (v + cubic_term * v * v * v))
    value = 0.5 * v * (1.0 + t)
    slope = 0.5 * (1.0 + t) + 0.5 * v * (1.0 - t * t) * root_two_pi * (
        1.0 + 3.0 * cubic_term * v * v
    )
    return value, slope


def column(ref, choice, rows):
    row = lax.broadcasted_iota(jnp.int32, (rows, LANES), 0)
    out = jnp.zeros((rows, LANES), jnp.int32)
    for r in range(rows):
        out = jnp.where(row == r, ref[choice, r], out)
    return out


def pack_kernel(ids, slots, kept, tok, grad, gain, router, *outs):
    messages, gates_ref = outs[:-1], outs[-1]
    rows, width = tok.shape
    experts = router.shape[0]
    pieces, tail, head = layout(rows, width)
    me = lax.axis_index("expert")
    x = tok[...].astype(jnp.float32)
    g = grad[...].astype(jnp.float32)
    inverse = lax.rsqrt(jnp.mean(x * x, axis=1, keepdims=True) + 1e-06)
    normed = (x * inverse * gain[...]).astype(jnp.bfloat16)
    wide = normed.astype(jnp.float32)
    id0, id1 = column(ids, 0, rows), column(ids, 1, rows)
    pick0 = jnp.zeros((rows, LANES), jnp.float32)
    pick1 = jnp.zeros((rows, LANES), jnp.float32)
    for e in range(experts):
        logit = jnp.sum(wide * router[e : e + 1, :].astype(jnp.float32), axis=1, keepdims=True)
        pick0 = jnp.where(id0 == e, logit, pick0)
        pick1 = jnp.where(id1 == e, logit, pick1)
    gate0 = 1.0 / (1.0 + jnp.exp(pick1 - pick0))
    gate1 = 1.0 / (1.0 + jnp.exp(pick0 - pick1))
    gates_ref[...] = jnp.zeros_like(gates_ref)
    gates_ref[0:rows, :] = gate0
    gates_ref[PAD : PAD + rows, :] = gate1
    row = lax.broadcasted_iota(jnp.int32, (PAD, LANES), 0)
    field = lax.broadcasted_iota(jnp.int32, (PAD, LANES), 1) // FIELD
    for k, out in enumerate(messages):
        expert = me ^ k
        gate = jnp.where(id0 == expert, gate0, jnp.where(id1 == expert, gate1, 0.0))
        weighted = (gate[:, 0:1] * g).astype(jnp.bfloat16).astype(jnp.float32)
        low = []
        for first in range(0, rows, pieces):
            last = [weighted[r : r + 1, width - tail :] for r in range(first, min(first + pieces, rows))]
            last += [jnp.zeros((1, tail), jnp.float32)] * (pieces - len(last))
            low.append(jnp.concatenate(last, axis=1))
        high = jnp.concatenate([wide, weighted[:, : width - tail]], axis=1)
        out[:, :head] = jnp.concatenate([high] + low, axis=0).astype(jnp.bfloat16)
        table = jnp.full((PAD, LANES), -1, jnp.int32)
        for r in range(rows):
            hit0 = (ids[0, r] == expert) & (kept[0, r] == 1)
            hit1 = (ids[1, r] == expert) & (kept[1, r] == 1)
            slot = jnp.where(hit0, slots[0, r], jnp.where(hit1, slots[1, r], -1))
            here = (row == r) & (field == 0)
            there = (row == rows + r // pieces) & (field == 1 + r % pieces)
            table = jnp.where(here | there, slot, table)
        out[:, head:] = table.astype(jnp.float32).astype(jnp.bfloat16)


def bin_kernel(rows, width, done, *refs):
    del done
    messages, (bins, placed_ref) = refs[:-2], refs[-2:]
    pieces, tail, head = layout(rows, width)
    arrived = jnp.concatenate([m[...].astype(jnp.float32) for m in messages], axis=0)
    lane = lax.broadcasted_iota(jnp.int32, (arrived.shape[0], LANES), 1) % FIELD
    placed = jnp.where(arrived[:, head:] == lane.astype(jnp.float32), 1.0, 0.0)
    placed_ref[...] = placed
    onehot = placed.T.astype(jnp.bfloat16)
    packed = arrived[:, :head].astype(jnp.bfloat16)
    first = jnp.dot(onehot[:SLOTS], packed, preferred_element_type=jnp.float32)
    bins[0:SLOTS, :] = first[:, :width].astype(jnp.bfloat16)
    bins[SLOTS : 2 * SLOTS, : width - tail] = first[:, width:].astype(jnp.bfloat16)
    rest = 0.0
    for p in range(pieces):
        which = onehot[(p + 1) * FIELD : (p + 1) * FIELD + SLOTS]
        rest += jnp.dot(
            which, packed[:, p * tail : (p + 1) * tail], preferred_element_type=jnp.float32
        )
    bins[SLOTS : 2 * SLOTS, width - tail :] = rest.astype(jnp.bfloat16)


def load_kernel(start, after, weight, out, done, sem):
    copy = pltpu.make_async_copy(weight.at[0, :, pl.ds(start, out.shape[1])], out, sem)
    copy.start()
    done[...] = after[0:8, :]
    copy.wait()


def expert_kernel(groups, *refs):
    pairs = refs[: groups // 2]
    up_a, up_b, down_hbm, keep, send, x, g, active, back_hidden, slope, down, sems = refs[
        groups // 2 :
    ]
    rows = groups * SLOTS
    width, early = up_a.shape
    hidden = early + up_b.shape[1]
    block = width // sems.shape[0]
    over = (((1,), (1,)), ((), ()))

    def fetch(i):
        at = pl.ds(i * block, block)
        return pltpu.make_async_copy(down_hbm.at[0, at, :], down.at[at, :], sems.at[i])

    for i in range(sems.shape[0]):
        fetch(i).start()
    x[...] = jnp.zeros_like(x)
    g[...] = jnp.zeros_like(g)
    for j in range(groups):
        pair, at = pairs[j % (groups // 2)], j // (groups // 2) * 2 * SLOTS
        x[j * SLOTS : (j + 1) * SLOTS, :] = pair[at : at + SLOTS, :]
        g[j * SLOTS : (j + 1) * SLOTS, :] = pair[at + SLOTS : at + 2 * SLOTS, :]

    def deliver(total, at, side):
        part = total.T.astype(jnp.bfloat16)
        for j in range(groups):
            to = send if j % 2 else keep
            row = (j // 2) * 2 * SLOTS + side * SLOTS
            to[row : row + SLOTS, at] = part[j * SLOTS : (j + 1) * SLOTS]

    taken = lax.axis_index("expert") >= 0

    @pl.when(taken)
    def _():
        for f in range(0, hidden, STEP):
            part, c = (up_a, f) if f < early else (up_b, f - early)
            v = jnp.dot(x[...], part[:, c : c + STEP], preferred_element_type=jnp.float32)
            value, rise = gelu_both(v[:rows])
            active[:, f : f + STEP] = value.astype(jnp.bfloat16)
            slope[:, f : f + STEP] = rise

    for i in range(sems.shape[0]):

        @pl.when(taken)
        def _(i=i):
            fetch(i).wait()
            for d in range(i * block, (i + 1) * block, STEP):
                total = lax.dot_general(
                    down[d : d + STEP, :], active[...], over, preferred_element_type=jnp.float32
                )
                deliver(total, slice(d, d + STEP), 0)

    for f in range(0, hidden, STEP):
        v = jnp.dot(g[...], down[:, f : f + STEP], preferred_element_type=jnp.float32)[:rows]
        back_hidden[:, f : f + STEP] = (v * slope[:, f : f + STEP]).astype(jnp.bfloat16)
    for d in range(0, width, STEP):
        total = lax.dot_general(
            up_a[d : d + STEP, :],
            back_hidden[:, :early],
            over,
            preferred_element_type=jnp.float32,
        )
        total += lax.dot_general(
            up_b[d : d + STEP, :],
            back_hidden[:, early:],
            over,
            preferred_element_type=jnp.float32,
        )
        deliver(total, slice(d, d + STEP), 1)


def join_kernel(done, a, b, out):
    del done
    out[0 : 2 * SLOTS, :] = a[...]
    out[2 * SLOTS :, :] = b[...]


def add_kernel(a, b, out):
    total = a[...].astype(jnp.float32) + b[...].astype(jnp.float32)
    out[...] = total.astype(jnp.bfloat16)


def reply_kernel(rows, n_parts, *refs):
    parts, placed, replies = refs[:n_parts], refs[n_parts], refs[n_parts + 1 :]
    width = parts[0].shape[1]
    pieces, tail, head = layout(rows, width)
    total = parts[0][0 : 2 * SLOTS, :].astype(jnp.float32)
    for p in parts[1:]:
        total = total + p[0 : 2 * SLOTS, :].astype(jnp.float32)
    total = total.astype(jnp.bfloat16)
    both = jnp.concatenate([total[:SLOTS], total[SLOTS:]], axis=1)
    onehot = placed[...].astype(jnp.bfloat16)
    for p in range(pieces):
        at = slice(p * tail, (p + 1) * tail)
        which = onehot[:, (p + 1) * FIELD : (p + 1) * FIELD + SLOTS]
        spread = jnp.dot(onehot[:, :SLOTS], both[:, at], preferred_element_type=jnp.float32)
        spread += jnp.dot(which, both[:, head:], preferred_element_type=jnp.float32)
        for k, out in enumerate(replies):
            out[:, at] = spread[k * PAD : (k + 1) * PAD].astype(jnp.bfloat16)


def finish_kernel(ids, tok, grad, gain, router, gates, *refs):
    replies, (mixed, grad_tokens) = refs[:-2], refs[-2:]
    rows, width = tok.shape
    experts = router.shape[0]
    pieces, tail, head = layout(rows, width)
    me = lax.axis_index("expert")
    x = tok[...].astype(jnp.float32)
    g = grad[...].astype(jnp.float32)
    inverse = lax.rsqrt(jnp.mean(x * x, axis=1, keepdims=True) + 1e-06)
    id0, id1 = column(ids, 0, rows)[:, 0:1], column(ids, 1, rows)[:, 0:1]
    gate0, gate1 = gates[0:rows, 0:1], gates[PAD : PAD + rows, 0:1]
    chosen0 = jnp.zeros((rows, width), jnp.float32)
    chosen1 = jnp.zeros((rows, width), jnp.float32)
    back = jnp.zeros((PAD, head), jnp.float32)
    for k, reply in enumerate(replies):
        expert = me ^ k
        answer = reply[...].astype(jnp.float32)
        chosen0 = jnp.where(id0 == expert, answer[:rows, :width], chosen0)
        chosen1 = jnp.where(id1 == expert, answer[:rows, :width], chosen1)
        back = back + answer
    rest = []
    for r in range(rows):
        p = r % pieces
        rest.append(back[rows + r // pieces : rows + r // pieces + 1, p * tail : (p + 1) * tail])
    back = jnp.concatenate([back[:rows, width:], jnp.concatenate(rest, axis=0)], axis=1)
    mixed[...] = (gate0 * chosen0 + gate1 * chosen1).astype(jnp.bfloat16)
    grad0 = jnp.sum(g * chosen0, axis=1, keepdims=True)
    grad1 = jnp.sum(g * chosen1, axis=1, keepdims=True)
    spread = gate0 * gate1 * (grad0 - grad1)
    for e in range(experts):
        line = router[e : e + 1, :].astype(jnp.float32)
        weight = jnp.where(id0 == e, spread, 0.0) - jnp.where(id1 == e, spread, 0.0)
        back = back + weight * line
    upstream = back * gain[...]
    mean = jnp.mean(upstream * x, axis=1, keepdims=True)
    grad_tokens[...] = (inverse * (upstream - x * inverse * inverse * mean)).astype(jnp.bfloat16)


def near(array):
    return pltpu.with_memory_space_constraint(array, pltpu.VMEM)


def far(array):
    return pltpu.with_memory_space_constraint(array, pltpu.HBM)


def call(body, out_shape, in_specs, args, limit=SMALL):
    return pl.pallas_call(
        body,
        out_shape=out_shape,
        in_specs=in_specs,
        out_specs=[VM] * len(out_shape),
        compiler_params=pltpu.CompilerParams(vmem_limit_bytes=limit),
    )(*args)


def shards(
    tokens, norm_gain, router, up_weight, down_weight, expert_ids, bin_slots, kept_mask, grad_out
):
    rows, width = tokens.shape
    hidden = up_weight.shape[2]
    experts = lax.axis_size("expert")
    groups = lax.axis_size("tensor")
    bf16, f32 = jnp.bfloat16, jnp.float32
    pieces, tail, head = layout(rows, width)

    def swap(array, axis, mask):
        n = lax.axis_size(axis)
        return lax.ppermute(array, axis, [(i, i ^ mask) for i in range(n)])

    ids, slots, kept = expert_ids.T, bin_slots.T, kept_mask.T
    gain, lines = norm_gain.reshape(1, width), router.T

    *messages, gates = call(
        pack_kernel,
        [pltpu.VMEM((PAD, head + LANES), bf16)] * experts
        + [pltpu.VMEM((2 * PAD, LANES), f32)],
        [SM] * 3 + [VM] * 4,
        (ids, slots, kept, tokens, grad_out, gain, lines),
        limit=None,
    )
    arrived = [messages[0]] + [swap(messages[k], "expert", k) for k in range(1, experts)]

    def load(start, stop, after):
        return pl.pallas_call(
            functools.partial(load_kernel, start),
            out_shape=[pltpu.VMEM((width, stop - start), bf16), pltpu.VMEM((8, LANES), f32)],
            in_specs=[VM, FAR],
            out_specs=[VM, VM],
            scratch_shapes=[pltpu.SemaphoreType.DMA],
            compiler_params=pltpu.CompilerParams(vmem_limit_bytes=2**20),
            cost_estimate=pl.CostEstimate(
                flops=0, bytes_accessed=width * (stop - start) * 4, transcendentals=0
            ),
        )(after, far(up_weight))

    early = max(STEP, hidden * 5 // 8 // STEP * STEP)
    up_a, done = load(0, early, near(gates))

    own, placed = call(
        functools.partial(bin_kernel, rows, width),
        [pltpu.VMEM((2 * SLOTS, width), bf16), pltpu.VMEM((experts * PAD, LANES), f32)],
        [VM] * (1 + experts),
        [near(a) for a in (done, *arrived)],
    )
    up_b, done = load(early, hidden, near(placed))

    mask = groups // 2
    pair = call(
        join_kernel,
        [pltpu.VMEM((4 * SLOTS, width), bf16)],
        [VM] * 3,
        [near(a) for a in (done, own, swap(own, "tensor", mask))],
    )[0]
    bins = {0: pair}
    mask //= 2
    while mask:
        bins.update({j | mask: swap(b, "tensor", mask) for j, b in bins.items()})
        mask //= 2

    tall = max(groups * SLOTS, 128)
    short = groups * SLOTS
    keep, send = pl.pallas_call(
        functools.partial(expert_kernel, groups),
        out_shape=[pltpu.VMEM((short, width), bf16)] * 2,
        in_specs=[VM] * (groups // 2 + 2) + [FAR],
        out_specs=[VM] * 2,
        scratch_shapes=[
            pltpu.VMEM((tall, width), bf16),
            pltpu.VMEM((tall, width), bf16),
            pltpu.VMEM((short, hidden), bf16),
            pltpu.VMEM((short, hidden), bf16),
            pltpu.VMEM((short, hidden), f32),
            pltpu.VMEM((width, hidden), bf16),
            pltpu.SemaphoreType.DMA((3,)),
        ],
        compiler_params=pltpu.CompilerParams(vmem_limit_bytes=32 * 2**20),
    )(*[near(bins[j]) for j in range(groups // 2)], near(up_a), near(up_b), far(down_weight))

    got = swap(send, "tensor", 1)
    piece = pltpu.VMEM((2 * SLOTS, width), bf16)
    firsts, sums = [keep, got], {}
    for i in range(1, groups // 2):
        at = slice(2 * SLOTS * i, 2 * SLOTS * (i + 1))
        sums[2 * i] = (keep[at].astype(f32) + got[at].astype(f32)).astype(bf16)
    mask = 2
    while mask < groups:
        came = {j ^ mask: swap(a, "tensor", mask) for j, a in sums.items() if j & mask}
        sums = {j: a for j, a in sums.items() if not j & mask}
        for j, a in came.items():
            if j == 0:
                firsts.append(a)
            else:
                sums[j] = call(add_kernel, [piece], [VM] * 2, (near(sums[j]), near(a)))[0]
        mask *= 2

    replies = call(
        functools.partial(reply_kernel, rows, len(firsts)),
        [pltpu.VMEM((PAD, head), bf16)] * experts,
        [VM] * (len(firsts) + 1),
        [near(a) for a in (*firsts, placed)],
    )
    answers = [replies[0]] + [swap(replies[k], "expert", k) for k in range(1, experts)]

    result = jax.ShapeDtypeStruct((rows, width), bf16)
    mixed, grad_tokens = call(
        finish_kernel,
        [result, result],
        [SM] + [VM] * (5 + experts),
        (ids, tokens, grad_out, gain, lines, near(gates), *[near(a) for a in answers]),
    )
    return mixed, grad_tokens


def solution(mesh):
    split = P(("dp", "expert", "tensor"), None)
    weights = P("expert", None, "tensor")
    return jax.shard_map(
        shards,
        mesh=mesh,
        in_specs=(split, P(), P(), weights, weights, split, split, split, split),
        out_specs=(split, split),
        check_vma=False,
    )
```

```python
import functools

import jax
import jax.numpy as jnp
from jax import lax
from jax.experimental import pallas as pl
from jax.experimental.pallas import tpu as pltpu
from jax.sharding import PartitionSpec as P

GCAP = 15
SLOTS = 16
PAD = 8
LANES = 128
STEP = 512
SMALL = 4 * 2**20
FIELD = 32

root_two_pi = 0.7978845608028654
cubic_term = 0.044715

VM = pl.BlockSpec(memory_space=pltpu.VMEM)
SM = pl.BlockSpec(memory_space=pltpu.SMEM)
FAR = pl.BlockSpec(memory_space=pltpu.HBM)


def layout(rows, width):
    spare = PAD - rows
    pieces = -(-rows // spare)
    tail = 2 * width // (pieces + 1)
    return pieces, tail, 2 * width - tail


def gelu_both(v):
    t = jnp.tanh(root_two_pi * (v + cubic_term * v * v * v))
    value = 0.5 * v * (1.0 + t)
    slope = 0.5 * (1.0 + t) + 0.5 * v * (1.0 - t * t) * root_two_pi * (
        1.0 + 3.0 * cubic_term * v * v
    )
    return value, slope


def column(ref, choice, rows):
    row = lax.broadcasted_iota(jnp.int32, (rows, LANES), 0)
    out = jnp.zeros((rows, LANES), jnp.int32)
    for r in range(rows):
        out = jnp.where(row == r, ref[choice, r], out)
    return out


def pack_kernel(ids, slots, kept, tok, grad, gain, router, *outs):
    messages, gates_ref = outs[:-1], outs[-1]
    rows, width = tok.shape
    experts = router.shape[0]
    pieces, tail, head = layout(rows, width)
    me = lax.axis_index("expert")
    x = tok[...].astype(jnp.float32)
    g = grad[...].astype(jnp.float32)
    inverse = lax.rsqrt(jnp.mean(x * x, axis=1, keepdims=True) + 1e-06)
    normed = (x * inverse * gain[...]).astype(jnp.bfloat16)
    wide = normed.astype(jnp.float32)
    id0, id1 = column(ids, 0, rows), column(ids, 1, rows)
    pick0 = jnp.zeros((rows, LANES), jnp.float32)
    pick1 = jnp.zeros((rows, LANES), jnp.float32)
    for e in range(experts):
        logit = jnp.sum(wide * router[e : e + 1, :].astype(jnp.float32), axis=1, keepdims=True)
        pick0 = jnp.where(id0 == e, logit, pick0)
        pick1 = jnp.where(id1 == e, logit, pick1)
    gate0 = 1.0 / (1.0 + jnp.exp(pick1 - pick0))
    gate1 = 1.0 / (1.0 + jnp.exp(pick0 - pick1))
    gates_ref[...] = jnp.zeros_like(gates_ref)
    gates_ref[0:rows, :] = gate0
    gates_ref[PAD : PAD + rows, :] = gate1
    row = lax.broadcasted_iota(jnp.int32, (PAD, LANES), 0)
    field = lax.broadcasted_iota(jnp.int32, (PAD, LANES), 1) // FIELD
    for k, out in enumerate(messages):
        expert = me ^ k
        gate = jnp.where(id0 == expert, gate0, jnp.where(id1 == expert, gate1, 0.0))
        weighted = (gate[:, 0:1] * g).astype(jnp.bfloat16).astype(jnp.float32)
        low = []
        for first in range(0, rows, pieces):
            last = [weighted[r : r + 1, width - tail :] for r in range(first, min(first + pieces, rows))]
            last += [jnp.zeros((1, tail), jnp.float32)] * (pieces - len(last))
            low.append(jnp.concatenate(last, axis=1))
        high = jnp.concatenate([wide, weighted[:, : width - tail]], axis=1)
        out[:, :head] = jnp.concatenate([high] + low, axis=0).astype(jnp.bfloat16)
        table = jnp.full((PAD, LANES), -1, jnp.int32)
        for r in range(rows):
            hit0 = (ids[0, r] == expert) & (kept[0, r] == 1)
            hit1 = (ids[1, r] == expert) & (kept[1, r] == 1)
            slot = jnp.where(hit0, slots[0, r], jnp.where(hit1, slots[1, r], -1))
            here = (row == r) & (field == 0)
            there = (row == rows + r // pieces) & (field == 1 + r % pieces)
            table = jnp.where(here | there, slot, table)
        out[:, head:] = table.astype(jnp.float32).astype(jnp.bfloat16)


def bin_kernel(rows, width, done, *refs):
    del done
    messages, (bins, placed_ref) = refs[:-2], refs[-2:]
    pieces, tail, head = layout(rows, width)
    arrived = jnp.concatenate([m[...].astype(jnp.float32) for m in messages], axis=0)
    lane = lax.broadcasted_iota(jnp.int32, (arrived.shape[0], LANES), 1) % FIELD
    placed = jnp.where(arrived[:, head:] == lane.astype(jnp.float32), 1.0, 0.0)
    placed_ref[...] = placed
    onehot = placed.T.astype(jnp.bfloat16)
    packed = arrived[:, :head].astype(jnp.bfloat16)
    first = jnp.dot(onehot[:SLOTS], packed, preferred_element_type=jnp.float32)
    bins[0:SLOTS, :] = first[:, :width].astype(jnp.bfloat16)
    bins[SLOTS : 2 * SLOTS, : width - tail] = first[:, width:].astype(jnp.bfloat16)
    rest = 0.0
    for p in range(pieces):
        which = onehot[(p + 1) * FIELD : (p + 1) * FIELD + SLOTS]
        rest += jnp.dot(
            which, packed[:, p * tail : (p + 1) * tail], preferred_element_type=jnp.float32
        )
    bins[SLOTS : 2 * SLOTS, width - tail :] = rest.astype(jnp.bfloat16)


def load_kernel(start, after, weight, out, done, sem):
    copy = pltpu.make_async_copy(weight.at[0, :, pl.ds(start, out.shape[1])], out, sem)
    copy.start()
    done[...] = after[0:8, :]
    copy.wait()


def expert_kernel(groups, *refs):
    pairs = refs[: groups // 2]
    (up_a_in, up_b_in, down_hbm, keep, send, up_a, up_b) = refs[groups // 2 : groups // 2 + 7]
    x, g, active, back_hidden, slope, down, sems = refs[groups // 2 + 7 :]
    del up_a_in, up_b_in
    rows = groups * SLOTS
    width, early = up_a.shape
    hidden = early + up_b.shape[1]
    block = width // sems.shape[0]
    over = (((1,), (1,)), ((), ()))

    def fetch(i):
        at = pl.ds(i * block, block)
        return pltpu.make_async_copy(down_hbm.at[0, at, :], down.at[at, :], sems.at[i])

    def columns(f):
        return (up_a, f) if f < early else (up_b, f - early)

    for i in range(sems.shape[0]):
        fetch(i).start()
    x[...] = jnp.zeros_like(x)
    g[...] = jnp.zeros_like(g)
    back_hidden[...] = jnp.zeros_like(back_hidden)
    for j in range(groups):
        pair, at = pairs[j % (groups // 2)], j // (groups // 2) * 2 * SLOTS
        x[j * SLOTS : (j + 1) * SLOTS, :] = pair[at : at + SLOTS, :]
        g[j * SLOTS : (j + 1) * SLOTS, :] = pair[at + SLOTS : at + 2 * SLOTS, :]

    def deliver(part, at, side):
        for j in range(groups):
            to = send if j % 2 else keep
            row = (j // 2) * 2 * SLOTS + side * SLOTS
            to[row : row + SLOTS, at] = part[j * SLOTS : (j + 1) * SLOTS]

    taken = lax.axis_index("expert") >= 0

    @pl.when(taken)
    def _():
        for f in range(0, hidden, STEP):
            part, c = columns(f)
            v = jnp.dot(x[...], part[:, c : c + STEP], preferred_element_type=jnp.float32)
            value, rise = gelu_both(v[:rows])
            active[:, f : f + STEP] = value.astype(jnp.bfloat16)
            slope[:, f : f + STEP] = rise

    waiting = [(d, f) for d in range(0, width, STEP) for f in range(0, hidden, STEP)]
    share = -(-len(waiting) * 2 * STEP // (2 * width + hidden))

    def turn(count):
        for _ in range(min(count, len(waiting))):
            d, f = waiting.pop()
            part, c = columns(f)
            part[d : d + STEP, c : c + STEP] = part[d : d + STEP, c : c + STEP].T

    for i in range(sems.shape[0]):

        @pl.when(taken)
        def _(i=i):
            fetch(i).wait()
            for d in range(i * block, (i + 1) * block, STEP):
                total = lax.dot_general(
                    down[d : d + STEP, :], active[...], over, preferred_element_type=jnp.float32
                )
                deliver(total.T.astype(jnp.bfloat16), slice(d, d + STEP), 0)
                turn(share)

    @pl.when(taken)
    def _():
        for f in range(0, hidden, STEP):
            v = jnp.dot(g[...], down[:, f : f + STEP], preferred_element_type=jnp.float32)[:rows]
            back_hidden[0:rows, f : f + STEP] = (v * slope[:, f : f + STEP]).astype(jnp.bfloat16)
            turn(-(-share // 2))
        turn(len(waiting))

    for d in range(0, width, STEP):
        total = 0.0
        for f in range(0, hidden, STEP):
            part, c = columns(f)
            total += jnp.dot(
                back_hidden[:, f : f + STEP],
                part[d : d + STEP, c : c + STEP],
                preferred_element_type=jnp.float32,
            )
        deliver(total.astype(jnp.bfloat16), slice(d, d + STEP), 1)


def join_kernel(done, a, b, out):
    del done
    out[0 : 2 * SLOTS, :] = a[...]
    out[2 * SLOTS :, :] = b[...]


def add_kernel(a, b, out):
    total = a[...].astype(jnp.float32) + b[...].astype(jnp.float32)
    out[...] = total.astype(jnp.bfloat16)


def reply_kernel(rows, n_parts, *refs):
    parts, placed, replies = refs[:n_parts], refs[n_parts], refs[n_parts + 1 :]
    width = parts[0].shape[1]
    pieces, tail, head = layout(rows, width)
    total = parts[0][0 : 2 * SLOTS, :].astype(jnp.float32)
    for p in parts[1:]:
        total = total + p[0 : 2 * SLOTS, :].astype(jnp.float32)
    total = total.astype(jnp.bfloat16)
    both = jnp.concatenate([total[:SLOTS], total[SLOTS:]], axis=1)
    onehot = placed[...].astype(jnp.bfloat16)
    for p in range(pieces):
        at = slice(p * tail, (p + 1) * tail)
        which = onehot[:, (p + 1) * FIELD : (p + 1) * FIELD + SLOTS]
        spread = jnp.dot(onehot[:, :SLOTS], both[:, at], preferred_element_type=jnp.float32)
        spread += jnp.dot(which, both[:, head:], preferred_element_type=jnp.float32)
        for k, out in enumerate(replies):
            out[:, at] = spread[k * PAD : (k + 1) * PAD].astype(jnp.bfloat16)


def finish_kernel(ids, tok, grad, gain, router, gates, *refs):
    replies, (mixed, grad_tokens) = refs[:-2], refs[-2:]
    rows, width = tok.shape
    experts = router.shape[0]
    pieces, tail, head = layout(rows, width)
    me = lax.axis_index("expert")
    x = tok[...].astype(jnp.float32)
    g = grad[...].astype(jnp.float32)
    inverse = lax.rsqrt(jnp.mean(x * x, axis=1, keepdims=True) + 1e-06)
    id0, id1 = column(ids, 0, rows)[:, 0:1], column(ids, 1, rows)[:, 0:1]
    gate0, gate1 = gates[0:rows, 0:1], gates[PAD : PAD + rows, 0:1]
    chosen0 = jnp.zeros((rows, width), jnp.float32)
    chosen1 = jnp.zeros((rows, width), jnp.float32)
    back = jnp.zeros((PAD, head), jnp.float32)
    for k, reply in enumerate(replies):
        expert = me ^ k
        answer = reply[...].astype(jnp.float32)
        chosen0 = jnp.where(id0 == expert, answer[:rows, :width], chosen0)
        chosen1 = jnp.where(id1 == expert, answer[:rows, :width], chosen1)
        back = back + answer
    rest = []
    for r in range(rows):
        p = r % pieces
        rest.append(back[rows + r // pieces : rows + r // pieces + 1, p * tail : (p + 1) * tail])
    back = jnp.concatenate([back[:rows, width:], jnp.concatenate(rest, axis=0)], axis=1)
    mixed[...] = (gate0 * chosen0 + gate1 * chosen1).astype(jnp.bfloat16)
    grad0 = jnp.sum(g * chosen0, axis=1, keepdims=True)
    grad1 = jnp.sum(g * chosen1, axis=1, keepdims=True)
    spread = gate0 * gate1 * (grad0 - grad1)
    for e in range(experts):
        line = router[e : e + 1, :].astype(jnp.float32)
        weight = jnp.where(id0 == e, spread, 0.0) - jnp.where(id1 == e, spread, 0.0)
        back = back + weight * line
    upstream = back * gain[...]
    mean = jnp.mean(upstream * x, axis=1, keepdims=True)
    grad_tokens[...] = (inverse * (upstream - x * inverse * inverse * mean)).astype(jnp.bfloat16)


def near(array):
    return pltpu.with_memory_space_constraint(array, pltpu.VMEM)


def far(array):
    return pltpu.with_memory_space_constraint(array, pltpu.HBM)


def call(body, out_shape, in_specs, args, limit=SMALL):
    return pl.pallas_call(
        body,
        out_shape=out_shape,
        in_specs=in_specs,
        out_specs=[VM] * len(out_shape),
        compiler_params=pltpu.CompilerParams(vmem_limit_bytes=limit),
    )(*args)


def shards(
    tokens, norm_gain, router, up_weight, down_weight, expert_ids, bin_slots, kept_mask, grad_out
):
    rows, width = tokens.shape
    hidden = up_weight.shape[2]
    experts = lax.axis_size("expert")
    groups = lax.axis_size("tensor")
    bf16, f32 = jnp.bfloat16, jnp.float32
    pieces, tail, head = layout(rows, width)

    def swap(array, axis, mask):
        n = lax.axis_size(axis)
        return lax.ppermute(array, axis, [(i, i ^ mask) for i in range(n)])

    ids, slots, kept = expert_ids.T, bin_slots.T, kept_mask.T
    gain, lines = norm_gain.reshape(1, width), router.T

    *messages, gates = call(
        pack_kernel,
        [pltpu.VMEM((PAD, head + LANES), bf16)] * experts
        + [pltpu.VMEM((2 * PAD, LANES), f32)],
        [SM] * 3 + [VM] * 4,
        (ids, slots, kept, tokens, grad_out, gain, lines),
        limit=None,
    )
    arrived = [messages[0]] + [swap(messages[k], "expert", k) for k in range(1, experts)]

    def load(start, stop, after):
        return pl.pallas_call(
            functools.partial(load_kernel, start),
            out_shape=[pltpu.VMEM((width, stop - start), bf16), pltpu.VMEM((8, LANES), f32)],
            in_specs=[VM, FAR],
            out_specs=[VM, VM],
            scratch_shapes=[pltpu.SemaphoreType.DMA],
            compiler_params=pltpu.CompilerParams(vmem_limit_bytes=2**20),
            cost_estimate=pl.CostEstimate(
                flops=0, bytes_accessed=width * (stop - start) * 4, transcendentals=0
            ),
        )(after, far(up_weight))

    early = max(STEP, hidden * 5 // 8 // STEP * STEP)
    up_a, done = load(0, early, near(gates))

    own, placed = call(
        functools.partial(bin_kernel, rows, width),
        [pltpu.VMEM((2 * SLOTS, width), bf16), pltpu.VMEM((experts * PAD, LANES), f32)],
        [VM] * (1 + experts),
        [near(a) for a in (done, *arrived)],
    )
    up_b, done = load(early, hidden, near(placed))

    mask = groups // 2
    pair = call(
        join_kernel,
        [pltpu.VMEM((4 * SLOTS, width), bf16)],
        [VM] * 3,
        [near(a) for a in (done, own, swap(own, "tensor", mask))],
    )[0]
    bins = {0: pair}
    mask //= 2
    while mask:
        bins.update({j | mask: swap(b, "tensor", mask) for j, b in bins.items()})
        mask //= 2

    tall = max(groups * SLOTS, 128)
    short = groups * SLOTS
    keep, send, _, _ = pl.pallas_call(
        functools.partial(expert_kernel, groups),
        out_shape=[pltpu.VMEM((short, width), bf16)] * 2
        + [pltpu.VMEM(up_a.shape, bf16), pltpu.VMEM(up_b.shape, bf16)],
        input_output_aliases={groups // 2: 2, groups // 2 + 1: 3},
        in_specs=[VM] * (groups // 2 + 2) + [FAR],
        out_specs=[VM] * 4,
        scratch_shapes=[
            pltpu.VMEM((tall, width), bf16),
            pltpu.VMEM((tall, width), bf16),
            pltpu.VMEM((short, hidden), bf16),
            pltpu.VMEM((tall, hidden), bf16),
            pltpu.VMEM((short, hidden), f32),
            pltpu.VMEM((width, hidden), bf16),
            pltpu.SemaphoreType.DMA((3,)),
        ],
        compiler_params=pltpu.CompilerParams(vmem_limit_bytes=32 * 2**20),
    )(*[near(bins[j]) for j in range(groups // 2)], near(up_a), near(up_b), far(down_weight))

    got = swap(send, "tensor", 1)
    piece = pltpu.VMEM((2 * SLOTS, width), bf16)
    firsts, sums = [keep, got], {}
    for i in range(1, groups // 2):
        at = slice(2 * SLOTS * i, 2 * SLOTS * (i + 1))
        sums[2 * i] = (keep[at].astype(f32) + got[at].astype(f32)).astype(bf16)
    mask = 2
    while mask < groups:
        came = {j ^ mask: swap(a, "tensor", mask) for j, a in sums.items() if j & mask}
        sums = {j: a for j, a in sums.items() if not j & mask}
        for j, a in came.items():
            if j == 0:
                firsts.append(a)
            else:
                sums[j] = call(add_kernel, [piece], [VM] * 2, (near(sums[j]), near(a)))[0]
        mask *= 2

    replies = call(
        functools.partial(reply_kernel, rows, len(firsts)),
        [pltpu.VMEM((PAD, head), bf16)] * experts,
        [VM] * (len(firsts) + 1),
        [near(a) for a in (*firsts, placed)],
    )
    answers = [replies[0]] + [swap(replies[k], "expert", k) for k in range(1, experts)]

    result = jax.ShapeDtypeStruct((rows, width), bf16)
    mixed, grad_tokens = call(
        finish_kernel,
        [result, result],
        [SM] + [VM] * (5 + experts),
        (ids, tokens, grad_out, gain, lines, near(gates), *[near(a) for a in answers]),
    )
    return mixed, grad_tokens


def solution(mesh):
    split = P(("dp", "expert", "tensor"), None)
    weights = P("expert", None, "tensor")
    return jax.shard_map(
        shards,
        mesh=mesh,
        in_specs=(split, P(), P(), weights, weights, split, split, split, split),
        out_specs=(split, split),
        check_vma=False,
    )
```

```python
import functools

import jax
import jax.numpy as jnp
from jax import lax
from jax.experimental import pallas as pl
from jax.experimental.pallas import tpu as pltpu
from jax.sharding import PartitionSpec as P

GCAP = 15
SLOTS = 16
PAD = 8
LANES = 128
STEP = 512
SMALL = 4 * 2**20
FIELD = 32

root_two_pi = 0.7978845608028654
cubic_term = 0.044715

VM = pl.BlockSpec(memory_space=pltpu.VMEM)
SM = pl.BlockSpec(memory_space=pltpu.SMEM)
FAR = pl.BlockSpec(memory_space=pltpu.HBM)


def layout(rows, width):
    spare = PAD - rows
    pieces = -(-rows // spare)
    tail = 2 * width // (pieces + 1)
    return pieces, tail, 2 * width - tail


def gelu_both(v):
    t = jnp.tanh(root_two_pi * (v + cubic_term * v * v * v))
    value = 0.5 * v * (1.0 + t)
    slope = 0.5 * (1.0 + t) + 0.5 * v * (1.0 - t * t) * root_two_pi * (
        1.0 + 3.0 * cubic_term * v * v
    )
    return value, slope


def column(ref, choice, rows):
    row = lax.broadcasted_iota(jnp.int32, (rows, LANES), 0)
    out = jnp.zeros((rows, LANES), jnp.int32)
    for r in range(rows):
        out = jnp.where(row == r, ref[choice, r], out)
    return out


def pack_kernel(ids, slots, kept, tok, grad, gain, router, *outs):
    messages, gates_ref = outs[:-1], outs[-1]
    rows, width = tok.shape
    experts = router.shape[0]
    pieces, tail, head = layout(rows, width)
    me = lax.axis_index("expert")
    x = tok[...].astype(jnp.float32)
    g = grad[...].astype(jnp.float32)
    inverse = lax.rsqrt(jnp.mean(x * x, axis=1, keepdims=True) + 1e-06)
    normed = (x * inverse * gain[...]).astype(jnp.bfloat16)
    wide = normed.astype(jnp.float32)
    id0, id1 = column(ids, 0, rows), column(ids, 1, rows)
    pick0 = jnp.zeros((rows, LANES), jnp.float32)
    pick1 = jnp.zeros((rows, LANES), jnp.float32)
    for e in range(experts):
        logit = jnp.sum(wide * router[e : e + 1, :].astype(jnp.float32), axis=1, keepdims=True)
        pick0 = jnp.where(id0 == e, logit, pick0)
        pick1 = jnp.where(id1 == e, logit, pick1)
    gate0 = 1.0 / (1.0 + jnp.exp(pick1 - pick0))
    gate1 = 1.0 / (1.0 + jnp.exp(pick0 - pick1))
    gates_ref[...] = jnp.zeros_like(gates_ref)
    gates_ref[0:rows, :] = gate0
    gates_ref[PAD : PAD + rows, :] = gate1
    row = lax.broadcasted_iota(jnp.int32, (PAD, LANES), 0)
    field = lax.broadcasted_iota(jnp.int32, (PAD, LANES), 1) // FIELD
    for k, out in enumerate(messages):
        expert = me ^ k
        gate = jnp.where(id0 == expert, gate0, jnp.where(id1 == expert, gate1, 0.0))
        weighted = (gate[:, 0:1] * g).astype(jnp.bfloat16).astype(jnp.float32)
        low = []
        for first in range(0, rows, pieces):
            last = [weighted[r : r + 1, width - tail :] for r in range(first, min(first + pieces, rows))]
            last += [jnp.zeros((1, tail), jnp.float32)] * (pieces - len(last))
            low.append(jnp.concatenate(last, axis=1))
        high = jnp.concatenate([wide, weighted[:, : width - tail]], axis=1)
        out[:, :head] = jnp.concatenate([high] + low, axis=0).astype(jnp.bfloat16)
        table = jnp.full((PAD, LANES), -1, jnp.int32)
        for r in range(rows):
            hit0 = (ids[0, r] == expert) & (kept[0, r] == 1)
            hit1 = (ids[1, r] == expert) & (kept[1, r] == 1)
            slot = jnp.where(hit0, slots[0, r], jnp.where(hit1, slots[1, r], -1))
            here = (row == r) & (field == 0)
            there = (row == rows + r // pieces) & (field == 1 + r % pieces)
            table = jnp.where(here | there, slot, table)
        out[:, head:] = table.astype(jnp.float32).astype(jnp.bfloat16)


def bin_kernel(rows, width, done, *refs):
    del done
    messages, (bins, placed_ref) = refs[:-2], refs[-2:]
    pieces, tail, head = layout(rows, width)
    arrived = jnp.concatenate([m[...].astype(jnp.float32) for m in messages], axis=0)
    lane = lax.broadcasted_iota(jnp.int32, (arrived.shape[0], LANES), 1) % FIELD
    placed = jnp.where(arrived[:, head:] == lane.astype(jnp.float32), 1.0, 0.0)
    placed_ref[...] = placed
    onehot = placed.T.astype(jnp.bfloat16)
    packed = arrived[:, :head].astype(jnp.bfloat16)
    first = jnp.dot(onehot[:SLOTS], packed, preferred_element_type=jnp.float32)
    bins[0:SLOTS, :] = first[:, :width].astype(jnp.bfloat16)
    bins[SLOTS : 2 * SLOTS, : width - tail] = first[:, width:].astype(jnp.bfloat16)
    rest = 0.0
    for p in range(pieces):
        which = onehot[(p + 1) * FIELD : (p + 1) * FIELD + SLOTS]
        rest += jnp.dot(
            which, packed[:, p * tail : (p + 1) * tail], preferred_element_type=jnp.float32
        )
    bins[SLOTS : 2 * SLOTS, width - tail :] = rest.astype(jnp.bfloat16)


def load_kernel(start, after, weight, out, done, sem):
    copy = pltpu.make_async_copy(weight.at[0, :, pl.ds(start, out.shape[1])], out, sem)
    copy.start()
    done[...] = after[0:8, :]
    copy.wait()


def expert_kernel(groups, *refs):
    bins, refs = refs[:groups], refs[groups:]
    _, _, down_hbm, up_a, up_b = refs[:5]
    outs, refs = refs[5 : 5 + groups], refs[5 + groups :]
    x, g, active, back_hidden, slope, down, sems = refs
    rows = groups * SLOTS
    width, early = up_a.shape
    hidden = early + up_b.shape[1]
    edges = [0, width // 3, width * 2 // 3, width]
    over = (((1,), (1,)), ((), ()))

    def fetch(i):
        at = pl.ds(edges[i], edges[i + 1] - edges[i])
        return pltpu.make_async_copy(down_hbm.at[0, at, :], down.at[at, :], sems.at[i])

    def columns(f):
        return (up_a, f) if f < early else (up_b, f - early)

    for i in range(len(edges) - 1):
        fetch(i).start()
    for j in range(groups):
        x[j * SLOTS : (j + 1) * SLOTS, :] = bins[j][0:SLOTS, :]
        g[j * SLOTS : (j + 1) * SLOTS, :] = bins[j][SLOTS : 2 * SLOTS, :]

    def deliver(part, at, side):
        for j, out in enumerate(outs):
            out[side * SLOTS : (side + 1) * SLOTS, at] = part[j * SLOTS : (j + 1) * SLOTS]

    taken = lax.axis_index("expert") >= 0

    @pl.when(taken)
    def _():
        for f in range(0, hidden, STEP):
            part, c = columns(f)
            v = jnp.dot(x[...], part[:, c : c + STEP], preferred_element_type=jnp.float32)
            value, rise = gelu_both(v[:rows])
            active[:, f : f + STEP] = value.astype(jnp.bfloat16)
            slope[:, f : f + STEP] = rise

    waiting = [(d, f) for d in range(0, width, STEP) for f in range(0, hidden, STEP)]
    share = -(-len(waiting) * 2 * STEP // (2 * width + hidden))

    def turn(count):
        for _ in range(min(count, len(waiting))):
            d, f = waiting.pop()
            part, c = columns(f)
            part[d : d + STEP, c : c + STEP] = part[d : d + STEP, c : c + STEP].T

    for i in range(len(edges) - 1):

        @pl.when(taken)
        def _(i=i):
            fetch(i).wait()
            for d in range(edges[i], edges[i + 1], STEP):
                total = lax.dot_general(
                    down[d : d + STEP, :], active[...], over, preferred_element_type=jnp.float32
                )
                deliver(total.T.astype(jnp.bfloat16), slice(d, d + STEP), 0)
                turn(share)

    @pl.when(taken)
    def _():
        for f in range(0, hidden, STEP):
            v = jnp.dot(g[...], down[:, f : f + STEP], preferred_element_type=jnp.float32)[:rows]
            back_hidden[0:rows, f : f + STEP] = (v * slope[:, f : f + STEP]).astype(jnp.bfloat16)
            turn(-(-share // 2))
        turn(len(waiting))

    for d in range(0, width, STEP):
        total = 0.0
        for f in range(0, hidden, STEP):
            part, c = columns(f)
            total += jnp.dot(
                back_hidden[:, f : f + STEP],
                part[d : d + STEP, c : c + STEP],
                preferred_element_type=jnp.float32,
            )
        deliver(total.astype(jnp.bfloat16), slice(d, d + STEP), 1)


def join_kernel(done, rows, out):
    del done
    out[...] = rows[...]


def add_kernel(a, b, out):
    total = a[...].astype(jnp.float32) + b[...].astype(jnp.float32)
    out[...] = total.astype(jnp.bfloat16)


def reply_kernel(rows, n_parts, *refs):
    parts, placed, replies = refs[:n_parts], refs[n_parts], refs[n_parts + 1 :]
    width = parts[0].shape[1]
    pieces, tail, head = layout(rows, width)
    total = parts[0][...].astype(jnp.float32)
    for p in parts[1:]:
        total = total + p[...].astype(jnp.float32)
    total = total.astype(jnp.bfloat16)
    both = jnp.concatenate([total[:SLOTS], total[SLOTS:]], axis=1)
    onehot = placed[...].astype(jnp.bfloat16)
    for p in range(pieces):
        at = slice(p * tail, (p + 1) * tail)
        which = onehot[:, (p + 1) * FIELD : (p + 1) * FIELD + SLOTS]
        spread = jnp.dot(onehot[:, :SLOTS], both[:, at], preferred_element_type=jnp.float32)
        spread += jnp.dot(which, both[:, head:], preferred_element_type=jnp.float32)
        for k, out in enumerate(replies):
            out[:, at] = spread[k * PAD : (k + 1) * PAD].astype(jnp.bfloat16)


def finish_kernel(ids, tok, grad, gain, router, gates, *refs):
    replies, (mixed, grad_tokens) = refs[:-2], refs[-2:]
    rows, width = tok.shape
    experts = router.shape[0]
    pieces, tail, head = layout(rows, width)
    me = lax.axis_index("expert")
    x = tok[...].astype(jnp.float32)
    g = grad[...].astype(jnp.float32)
    inverse = lax.rsqrt(jnp.mean(x * x, axis=1, keepdims=True) + 1e-06)
    id0, id1 = column(ids, 0, rows)[:, 0:1], column(ids, 1, rows)[:, 0:1]
    gate0, gate1 = gates[0:rows, 0:1], gates[PAD : PAD + rows, 0:1]
    chosen0 = jnp.zeros((rows, width), jnp.float32)
    chosen1 = jnp.zeros((rows, width), jnp.float32)
    back = jnp.zeros((PAD, head), jnp.float32)
    for k, reply in enumerate(replies):
        expert = me ^ k
        answer = reply[...].astype(jnp.float32)
        chosen0 = jnp.where(id0 == expert, answer[:rows, :width], chosen0)
        chosen1 = jnp.where(id1 == expert, answer[:rows, :width], chosen1)
        back = back + answer
    rest = []
    for r in range(rows):
        p = r % pieces
        rest.append(back[rows + r // pieces : rows + r // pieces + 1, p * tail : (p + 1) * tail])
    back = jnp.concatenate([back[:rows, width:], jnp.concatenate(rest, axis=0)], axis=1)
    mixed[...] = (gate0 * chosen0 + gate1 * chosen1).astype(jnp.bfloat16)
    grad0 = jnp.sum(g * chosen0, axis=1, keepdims=True)
    grad1 = jnp.sum(g * chosen1, axis=1, keepdims=True)
    spread = gate0 * gate1 * (grad0 - grad1)
    for e in range(experts):
        line = router[e : e + 1, :].astype(jnp.float32)
        weight = jnp.where(id0 == e, spread, 0.0) - jnp.where(id1 == e, spread, 0.0)
        back = back + weight * line
    upstream = back * gain[...]
    mean = jnp.mean(upstream * x, axis=1, keepdims=True)
    grad_tokens[...] = (inverse * (upstream - x * inverse * inverse * mean)).astype(jnp.bfloat16)


def near(array):
    return pltpu.with_memory_space_constraint(array, pltpu.VMEM)


def far(array):
    return pltpu.with_memory_space_constraint(array, pltpu.HBM)


def call(body, out_shape, in_specs, args, limit=SMALL):
    return pl.pallas_call(
        body,
        out_shape=out_shape,
        in_specs=in_specs,
        out_specs=[VM] * len(out_shape),
        compiler_params=pltpu.CompilerParams(vmem_limit_bytes=limit),
    )(*args)


def shards(
    tokens, norm_gain, router, up_weight, down_weight, expert_ids, bin_slots, kept_mask, grad_out
):
    rows, width = tokens.shape
    hidden = up_weight.shape[2]
    experts = lax.axis_size("expert")
    groups = lax.axis_size("tensor")
    bf16, f32 = jnp.bfloat16, jnp.float32
    pieces, tail, head = layout(rows, width)

    def swap(array, axis, mask):
        n = lax.axis_size(axis)
        return lax.ppermute(array, axis, [(i, i ^ mask) for i in range(n)])

    ids, slots, kept = expert_ids.T, bin_slots.T, kept_mask.T
    gain, lines = norm_gain.reshape(1, width), router.T

    *messages, gates = call(
        pack_kernel,
        [pltpu.VMEM((PAD, head + LANES), bf16)] * experts
        + [pltpu.VMEM((2 * PAD, LANES), f32)],
        [SM] * 3 + [VM] * 4,
        (ids, slots, kept, tokens, grad_out, gain, lines),
        limit=None,
    )
    arrived = [messages[0]] + [swap(messages[k], "expert", k) for k in range(1, experts)]

    def load(start, stop, after):
        return pl.pallas_call(
            functools.partial(load_kernel, start),
            out_shape=[pltpu.VMEM((width, stop - start), bf16), pltpu.VMEM((8, LANES), f32)],
            in_specs=[VM, FAR],
            out_specs=[VM, VM],
            scratch_shapes=[pltpu.SemaphoreType.DMA],
            compiler_params=pltpu.CompilerParams(vmem_limit_bytes=2**20),
            cost_estimate=pl.CostEstimate(
                flops=0, bytes_accessed=width * (stop - start) * 4, transcendentals=0
            ),
        )(after, far(up_weight))

    early = max(STEP, hidden * 5 // 8 // STEP * STEP)
    up_a, done = load(0, early, near(gates))

    own, placed = call(
        functools.partial(bin_kernel, rows, width),
        [pltpu.VMEM((2 * SLOTS, width), bf16), pltpu.VMEM((experts * PAD, LANES), f32)],
        [VM] * (1 + experts),
        [near(a) for a in (done, *arrived)],
    )
    up_b, done = load(early, hidden, near(placed))

    mask = groups // 2
    far_rows = call(
        join_kernel,
        [pltpu.VMEM((2 * SLOTS, width), bf16)],
        [VM] * 2,
        [near(a) for a in (done, swap(own, "tensor", mask))],
    )[0]
    bins = {0: own, mask: far_rows}
    mask //= 2
    while mask:
        bins.update({j | mask: swap(b, "tensor", mask) for j, b in bins.items()})
        mask //= 2

    tall = max(groups * SLOTS, 128)
    short = groups * SLOTS
    _, _, *sums = pl.pallas_call(
        functools.partial(expert_kernel, groups),
        out_shape=[pltpu.VMEM(up_a.shape, bf16), pltpu.VMEM(up_b.shape, bf16)]
        + [pltpu.VMEM((2 * SLOTS, width), bf16)] * groups,
        input_output_aliases={groups: 0, groups + 1: 1},
        in_specs=[VM] * (groups + 2) + [FAR],
        out_specs=[VM] * (groups + 2),
        scratch_shapes=[
            pltpu.VMEM((tall, width), bf16),
            pltpu.VMEM((tall, width), bf16),
            pltpu.VMEM((short, hidden), bf16),
            pltpu.VMEM((tall, hidden), bf16),
            pltpu.VMEM((short, hidden), f32),
            pltpu.VMEM((width, hidden), bf16),
            pltpu.SemaphoreType.DMA((3,)),
        ],
        compiler_params=pltpu.CompilerParams(vmem_limit_bytes=32 * 2**20),
    )(*[near(bins[j]) for j in range(groups)], near(up_a), near(up_b), far(down_weight))

    piece = pltpu.VMEM((2 * SLOTS, width), bf16)
    firsts = [sums[0], swap(sums[1], "tensor", 1)]
    sums = {
        j: (sums[j].astype(f32) + swap(sums[j + 1], "tensor", 1).astype(f32)).astype(bf16)
        for j in range(2, groups, 2)
    }
    mask = 2
    while mask < groups:
        came = {j ^ mask: swap(a, "tensor", mask) for j, a in sums.items() if j & mask}
        sums = {j: a for j, a in sums.items() if not j & mask}
        for j, a in came.items():
            if j == 0:
                firsts.append(a)
            else:
                sums[j] = call(add_kernel, [piece], [VM] * 2, (near(sums[j]), near(a)))[0]
        mask *= 2

    replies = call(
        functools.partial(reply_kernel, rows, len(firsts)),
        [pltpu.VMEM((PAD, head), bf16)] * experts,
        [VM] * (len(firsts) + 1),
        [near(a) for a in (*firsts, placed)],
    )
    answers = [replies[0]] + [swap(replies[k], "expert", k) for k in range(1, experts)]

    result = jax.ShapeDtypeStruct((rows, width), bf16)
    mixed, grad_tokens = call(
        finish_kernel,
        [result, result],
        [SM] + [VM] * (5 + experts),
        (ids, tokens, grad_out, gain, lines, near(gates), *[near(a) for a in answers]),
    )
    return mixed, grad_tokens


def solution(mesh):
    split = P(("dp", "expert", "tensor"), None)
    weights = P("expert", None, "tensor")
    return jax.shard_map(
        shards,
        mesh=mesh,
        in_specs=(split, P(), P(), weights, weights, split, split, split, split),
        out_specs=(split, split),
        check_vma=False,
    )
```

```python
import functools

import jax
import jax.numpy as jnp
from jax import lax
from jax.experimental import pallas as pl
from jax.experimental.pallas import tpu as pltpu
from jax.sharding import PartitionSpec as P

GCAP = 15
SLOTS = 16
PAD = 8
LANES = 128
STEP = 512
SMALL = 4 * 2**20
FIELD = 32

root_two_pi = 0.7978845608028654
cubic_term = 0.044715

VM = pl.BlockSpec(memory_space=pltpu.VMEM)
SM = pl.BlockSpec(memory_space=pltpu.SMEM)
FAR = pl.BlockSpec(memory_space=pltpu.HBM)


def layout(rows, width):
    spare = PAD - rows
    pieces = -(-rows // spare)
    tail = 2 * width // (pieces + 1)
    return pieces, tail, 2 * width - tail


def gelu_both(v):
    t = jnp.tanh(root_two_pi * (v + cubic_term * v * v * v))
    value = 0.5 * v * (1.0 + t)
    slope = 0.5 * (1.0 + t) + 0.5 * v * (1.0 - t * t) * root_two_pi * (
        1.0 + 3.0 * cubic_term * v * v
    )
    return value, slope


def column(ref, choice, rows):
    row = lax.broadcasted_iota(jnp.int32, (rows, LANES), 0)
    out = jnp.zeros((rows, LANES), jnp.int32)
    for r in range(rows):
        out = jnp.where(row == r, ref[choice, r], out)
    return out


def pack_kernel(ids, slots, kept, tok, grad, gain, router, *outs):
    messages, (gates_ref, tok_out, grad_out, gain_out, router_out) = outs[:-5], outs[-5:]
    rows, width = tok.shape
    experts = router.shape[0]
    pieces, tail, head = layout(rows, width)
    me = lax.axis_index("expert")
    x = tok[...].astype(jnp.float32)
    g = grad[...].astype(jnp.float32)
    inverse = lax.rsqrt(jnp.mean(x * x, axis=1, keepdims=True) + 1e-06)
    normed = (x * inverse * gain[...]).astype(jnp.bfloat16)
    wide = normed.astype(jnp.float32)
    id0, id1 = column(ids, 0, rows), column(ids, 1, rows)
    pick0 = jnp.zeros((rows, LANES), jnp.float32)
    pick1 = jnp.zeros((rows, LANES), jnp.float32)
    for e in range(experts):
        logit = jnp.sum(wide * router[e : e + 1, :].astype(jnp.float32), axis=1, keepdims=True)
        pick0 = jnp.where(id0 == e, logit, pick0)
        pick1 = jnp.where(id1 == e, logit, pick1)
    gate0 = 1.0 / (1.0 + jnp.exp(pick1 - pick0))
    gate1 = 1.0 / (1.0 + jnp.exp(pick0 - pick1))
    gates_ref[...] = jnp.zeros_like(gates_ref)
    kept_for_later = (gate0, gate1, id0.astype(jnp.float32), id1.astype(jnp.float32), inverse)
    for i, entry in enumerate(kept_for_later):
        gates_ref[i * PAD : i * PAD + rows, :] = jnp.broadcast_to(entry, (rows, LANES))
    tok_out[...] = tok[...]
    grad_out[...] = grad[...]
    gain_out[...] = gain[...]
    router_out[...] = router[...]
    row = lax.broadcasted_iota(jnp.int32, (PAD, LANES), 0)
    field = lax.broadcasted_iota(jnp.int32, (PAD, LANES), 1) // FIELD
    for k, out in enumerate(messages):
        expert = me ^ k
        gate = jnp.where(id0 == expert, gate0, jnp.where(id1 == expert, gate1, 0.0))
        weighted = (gate[:, 0:1] * g).astype(jnp.bfloat16).astype(jnp.float32)
        low = []
        for first in range(0, rows, pieces):
            last = [weighted[r : r + 1, width - tail :] for r in range(first, min(first + pieces, rows))]
            last += [jnp.zeros((1, tail), jnp.float32)] * (pieces - len(last))
            low.append(jnp.concatenate(last, axis=1))
        high = jnp.concatenate([wide, weighted[:, : width - tail]], axis=1)
        out[:, :head] = jnp.concatenate([high] + low, axis=0).astype(jnp.bfloat16)
        table = jnp.full((PAD, LANES), -1, jnp.int32)
        for r in range(rows):
            hit0 = (ids[0, r] == expert) & (kept[0, r] == 1)
            hit1 = (ids[1, r] == expert) & (kept[1, r] == 1)
            slot = jnp.where(hit0, slots[0, r], jnp.where(hit1, slots[1, r], -1))
            here = (row == r) & (field == 0)
            there = (row == rows + r // pieces) & (field == 1 + r % pieces)
            table = jnp.where(here | there, slot, table)
        out[:, head:] = table.astype(jnp.float32).astype(jnp.bfloat16)


def bin_kernel(rows, width, done, *refs):
    del done
    messages, (bins, placed_ref) = refs[:-2], refs[-2:]
    pieces, tail, head = layout(rows, width)
    arrived = jnp.concatenate([m[...].astype(jnp.float32) for m in messages], axis=0)
    lane = lax.broadcasted_iota(jnp.int32, (arrived.shape[0], LANES), 1) % FIELD
    placed = jnp.where(arrived[:, head:] == lane.astype(jnp.float32), 1.0, 0.0)
    placed_ref[...] = placed
    onehot = placed.T.astype(jnp.bfloat16)
    packed = arrived[:, :head].astype(jnp.bfloat16)
    first = jnp.dot(onehot[:SLOTS], packed, preferred_element_type=jnp.float32)
    bins[0:SLOTS, :] = first[:, :width].astype(jnp.bfloat16)
    bins[SLOTS : 2 * SLOTS, : width - tail] = first[:, width:].astype(jnp.bfloat16)
    rest = 0.0
    for p in range(pieces):
        which = onehot[(p + 1) * FIELD : (p + 1) * FIELD + SLOTS]
        rest += jnp.dot(
            which, packed[:, p * tail : (p + 1) * tail], preferred_element_type=jnp.float32
        )
    bins[SLOTS : 2 * SLOTS, width - tail :] = rest.astype(jnp.bfloat16)


def later(gates, i, rows):
    return gates[i * PAD : i * PAD + rows, 0:1]


def prepare_kernel(start, gates, tok, gain, router, weight, out, done, *refs):
    scale, along, share, fixed, mean, sem = refs
    copy = pltpu.make_async_copy(weight.at[0, :, pl.ds(start, out.shape[1])], out, sem)
    copy.start()
    done[...] = gates[0:8, :]
    rows, width = tok.shape
    id0, id1, inverse = (later(gates, i, rows) for i in (2, 3, 4))
    x = tok[...].astype(jnp.float32)
    line = jnp.zeros((rows, width), jnp.float32)
    for e in range(router.shape[0]):
        sign = jnp.where(id0 == e, 1.0, 0.0) - jnp.where(id1 == e, 1.0, 0.0)
        line = line + sign * router[e : e + 1, :].astype(jnp.float32)
    scaled = gain[...] * inverse
    weighted = gain[...] * x
    scale[...] = scaled
    along[...] = x * inverse * inverse * inverse
    share[...] = weighted
    fixed[...] = line * scaled
    total = jnp.mean(line * weighted, axis=1, keepdims=True)
    mean[...] = jnp.broadcast_to(total, mean.shape)
    copy.wait()


def load_kernel(start, after, weight, out, done, sem):
    copy = pltpu.make_async_copy(weight.at[0, :, pl.ds(start, out.shape[1])], out, sem)
    copy.start()
    done[...] = after[0:8, :]
    copy.wait()


def expert_kernel(groups, *refs):
    bins, refs = refs[:groups], refs[groups:]
    _, _, down_hbm, up_a, up_b = refs[:5]
    outs, refs = refs[5 : 5 + groups], refs[5 + groups :]
    x, g, active, back_hidden, slope, down, sems = refs
    rows = groups * SLOTS
    width, early = up_a.shape
    hidden = early + up_b.shape[1]
    edges = [0, width // 3, width * 2 // 3, width]
    over = (((1,), (1,)), ((), ()))

    def fetch(i):
        at = pl.ds(edges[i], edges[i + 1] - edges[i])
        return pltpu.make_async_copy(down_hbm.at[0, at, :], down.at[at, :], sems.at[i])

    def columns(f):
        return (up_a, f) if f < early else (up_b, f - early)

    for i in range(len(edges) - 1):
        fetch(i).start()
    for j in range(groups):
        x[j * SLOTS : (j + 1) * SLOTS, :] = bins[j][0:SLOTS, :]
        g[j * SLOTS : (j + 1) * SLOTS, :] = bins[j][SLOTS : 2 * SLOTS, :]

    def deliver(part, at, side):
        for j, out in enumerate(outs):
            out[side * SLOTS : (side + 1) * SLOTS, at] = part[j * SLOTS : (j + 1) * SLOTS]

    taken = lax.axis_index("expert") >= 0

    @pl.when(taken)
    def _():
        for f in range(0, hidden, STEP):
            part, c = columns(f)
            v = jnp.dot(x[...], part[:, c : c + STEP], preferred_element_type=jnp.float32)
            value, rise = gelu_both(v[:rows])
            active[:, f : f + STEP] = value.astype(jnp.bfloat16)
            slope[:, f : f + STEP] = rise

    waiting = [(d, f) for d in range(0, width, STEP) for f in range(0, hidden, STEP)]
    share = -(-len(waiting) * 2 * STEP // (2 * width + hidden))

    def turn(count):
        for _ in range(min(count, len(waiting))):
            d, f = waiting.pop()
            part, c = columns(f)
            part[d : d + STEP, c : c + STEP] = part[d : d + STEP, c : c + STEP].T

    for i in range(len(edges) - 1):

        @pl.when(taken)
        def _(i=i):
            fetch(i).wait()
            for d in range(edges[i], edges[i + 1], STEP):
                total = lax.dot_general(
                    down[d : d + STEP, :], active[...], over, preferred_element_type=jnp.float32
                )
                deliver(total.T.astype(jnp.bfloat16), slice(d, d + STEP), 0)
                turn(share)

    @pl.when(taken)
    def _():
        for f in range(0, hidden, STEP):
            v = jnp.dot(g[...], down[:, f : f + STEP], preferred_element_type=jnp.float32)[:rows]
            back_hidden[0:rows, f : f + STEP] = (v * slope[:, f : f + STEP]).astype(jnp.bfloat16)
            turn(-(-share // 2))
        turn(len(waiting))

    for d in range(0, width, STEP):
        total = 0.0
        for f in range(0, hidden, STEP):
            part, c = columns(f)
            total += jnp.dot(
                back_hidden[:, f : f + STEP],
                part[d : d + STEP, c : c + STEP],
                preferred_element_type=jnp.float32,
            )
        deliver(total.astype(jnp.bfloat16), slice(d, d + STEP), 1)


def join_kernel(done, rows, out):
    del done
    out[...] = rows[...]


def add_kernel(a, b, out):
    total = a[...].astype(jnp.float32) + b[...].astype(jnp.float32)
    out[...] = total.astype(jnp.bfloat16)


def reply_kernel(rows, n_parts, *refs):
    parts, placed, replies = refs[:n_parts], refs[n_parts], refs[n_parts + 1 :]
    width = parts[0].shape[1]
    pieces, tail, head = layout(rows, width)
    total = parts[0][...].astype(jnp.float32)
    for p in parts[1:]:
        total = total + p[...].astype(jnp.float32)
    total = total.astype(jnp.bfloat16)
    both = jnp.concatenate([total[:SLOTS], total[SLOTS:]], axis=1)
    onehot = placed[...].astype(jnp.bfloat16)
    for p in range(pieces):
        at = slice(p * tail, (p + 1) * tail)
        which = onehot[:, (p + 1) * FIELD : (p + 1) * FIELD + SLOTS]
        spread = jnp.dot(onehot[:, :SLOTS], both[:, at], preferred_element_type=jnp.float32)
        spread += jnp.dot(which, both[:, head:], preferred_element_type=jnp.float32)
        for k, out in enumerate(replies):
            out[:, at] = spread[k * PAD : (k + 1) * PAD].astype(jnp.bfloat16)


def finish_kernel(grad, gates, scale, along, share, fixed, fixed_mean, *refs):
    replies, (mixed, grad_tokens) = refs[:-2], refs[-2:]
    rows, width = grad.shape
    pieces, tail, head = layout(rows, width)
    me = lax.axis_index("expert")
    gate0, gate1, id0, id1 = (later(gates, i, rows) for i in range(4))
    chosen0 = jnp.zeros((rows, width), jnp.float32)
    chosen1 = jnp.zeros((rows, width), jnp.float32)
    back = jnp.zeros((PAD, head), jnp.float32)
    for k, reply in enumerate(replies):
        expert = (me ^ k).astype(jnp.float32)
        answer = reply[...].astype(jnp.float32)
        chosen0 = jnp.where(id0 == expert, answer[:rows, :width], chosen0)
        chosen1 = jnp.where(id1 == expert, answer[:rows, :width], chosen1)
        back = back + answer
    rest = []
    for r in range(rows):
        p = r % pieces
        rest.append(back[rows + r // pieces : rows + r // pieces + 1, p * tail : (p + 1) * tail])
    back = jnp.concatenate([back[:rows, width:], jnp.concatenate(rest, axis=0)], axis=1)
    mixed[...] = (gate0 * chosen0 + gate1 * chosen1).astype(jnp.bfloat16)
    g = grad[...].astype(jnp.float32)
    spread = gate0 * gate1 * jnp.sum(g * (chosen0 - chosen1), axis=1, keepdims=True)
    mean = jnp.mean(back * share[...], axis=1, keepdims=True) + spread * fixed_mean[:, 0:1]
    grad_tokens[...] = (
        back * scale[...] + spread * fixed[...] - along[...] * mean
    ).astype(jnp.bfloat16)


def near(array):
    return pltpu.with_memory_space_constraint(array, pltpu.VMEM)


def far(array):
    return pltpu.with_memory_space_constraint(array, pltpu.HBM)


def call(body, out_shape, in_specs, args, limit=SMALL):
    return pl.pallas_call(
        body,
        out_shape=out_shape,
        in_specs=in_specs,
        out_specs=[VM] * len(out_shape),
        compiler_params=pltpu.CompilerParams(vmem_limit_bytes=limit),
    )(*args)


def shards(
    tokens, norm_gain, router, up_weight, down_weight, expert_ids, bin_slots, kept_mask, grad_out
):
    rows, width = tokens.shape
    hidden = up_weight.shape[2]
    experts = lax.axis_size("expert")
    groups = lax.axis_size("tensor")
    bf16, f32 = jnp.bfloat16, jnp.float32
    pieces, tail, head = layout(rows, width)

    def swap(array, axis, mask):
        n = lax.axis_size(axis)
        return lax.ppermute(array, axis, [(i, i ^ mask) for i in range(n)])

    ids, slots, kept = expert_ids.T, bin_slots.T, kept_mask.T
    gain, lines = norm_gain.reshape(1, width), router.T

    *messages, gates, tokens, grad_out, gain, lines = call(
        pack_kernel,
        [pltpu.VMEM((PAD, head + LANES), bf16)] * experts
        + [pltpu.VMEM((5 * PAD, LANES), f32)]
        + [pltpu.VMEM(a.shape, a.dtype) for a in (tokens, grad_out, gain, lines)],
        [SM] * 3 + [VM] * 4,
        (ids, slots, kept, tokens, grad_out, gain, lines),
        limit=None,
    )
    arrived = [messages[0]] + [swap(messages[k], "expert", k) for k in range(1, experts)]

    def load(body, start, stop, given, more):
        return pl.pallas_call(
            functools.partial(body, start),
            out_shape=[pltpu.VMEM((width, stop - start), bf16), pltpu.VMEM((8, LANES), f32)]
            + more,
            in_specs=[VM] * len(given) + [FAR],
            out_specs=[VM] * (2 + len(more)),
            scratch_shapes=[pltpu.SemaphoreType.DMA],
            compiler_params=pltpu.CompilerParams(vmem_limit_bytes=2**20),
            cost_estimate=pl.CostEstimate(
                flops=0, bytes_accessed=width * (stop - start) * 4, transcendentals=0
            ),
        )(*[near(a) for a in given], far(up_weight))

    early = max(STEP, hidden * 5 // 8 // STEP * STEP)
    up_a, done, *factors = load(
        prepare_kernel,
        0,
        early,
        (gates, tokens, gain, lines),
        [pltpu.VMEM((rows, width), f32)] * 4 + [pltpu.VMEM((rows, LANES), f32)],
    )

    own, placed = call(
        functools.partial(bin_kernel, rows, width),
        [pltpu.VMEM((2 * SLOTS, width), bf16), pltpu.VMEM((experts * PAD, LANES), f32)],
        [VM] * (1 + experts),
        [near(a) for a in (done, *arrived)],
    )
    up_b, done = load(load_kernel, early, hidden, (placed,), [])

    mask = groups // 2
    far_rows = call(
        join_kernel,
        [pltpu.VMEM((2 * SLOTS, width), bf16)],
        [VM] * 2,
        [near(a) for a in (done, swap(own, "tensor", mask))],
    )[0]
    bins = {0: own, mask: far_rows}
    mask //= 2
    while mask:
        bins.update({j | mask: swap(b, "tensor", mask) for j, b in bins.items()})
        mask //= 2

    tall = max(groups * SLOTS, 128)
    short = groups * SLOTS
    _, _, *sums = pl.pallas_call(
        functools.partial(expert_kernel, groups),
        out_shape=[pltpu.VMEM(up_a.shape, bf16), pltpu.VMEM(up_b.shape, bf16)]
        + [pltpu.VMEM((2 * SLOTS, width), bf16)] * groups,
        input_output_aliases={groups: 0, groups + 1: 1},
        in_specs=[VM] * (groups + 2) + [FAR],
        out_specs=[VM] * (groups + 2),
        scratch_shapes=[
            pltpu.VMEM((tall, width), bf16),
            pltpu.VMEM((tall, width), bf16),
            pltpu.VMEM((short, hidden), bf16),
            pltpu.VMEM((tall, hidden), bf16),
            pltpu.VMEM((short, hidden), f32),
            pltpu.VMEM((width, hidden), bf16),
            pltpu.SemaphoreType.DMA((3,)),
        ],
        compiler_params=pltpu.CompilerParams(vmem_limit_bytes=32 * 2**20),
    )(*[near(bins[j]) for j in range(groups)], near(up_a), near(up_b), far(down_weight))

    piece = pltpu.VMEM((2 * SLOTS, width), bf16)
    firsts = [sums[0], swap(sums[1], "tensor", 1)]
    sums = {
        j: (sums[j].astype(f32) + swap(sums[j + 1], "tensor", 1).astype(f32)).astype(bf16)
        for j in range(2, groups, 2)
    }
    mask = 2
    while mask < groups:
        came = {j ^ mask: swap(a, "tensor", mask) for j, a in sums.items() if j & mask}
        sums = {j: a for j, a in sums.items() if not j & mask}
        for j, a in came.items():
            if j == 0:
                firsts.append(a)
            else:
                sums[j] = call(add_kernel, [piece], [VM] * 2, (near(sums[j]), near(a)))[0]
        mask *= 2

    replies = call(
        functools.partial(reply_kernel, rows, len(firsts)),
        [pltpu.VMEM((PAD, head), bf16)] * experts,
        [VM] * (len(firsts) + 1),
        [near(a) for a in (*firsts, placed)],
    )
    answers = [replies[0]] + [swap(replies[k], "expert", k) for k in range(1, experts)]

    result = jax.ShapeDtypeStruct((rows, width), bf16)
    mixed, grad_tokens = call(
        finish_kernel,
        [result, result],
        [VM] * (7 + experts),
        [near(a) for a in (grad_out, gates, *factors, *answers)],
    )
    return mixed, grad_tokens


def solution(mesh):
    split = P(("dp", "expert", "tensor"), None)
    weights = P("expert", None, "tensor")
    return jax.shard_map(
        shards,
        mesh=mesh,
        in_specs=(split, P(), P(), weights, weights, split, split, split, split),
        out_specs=(split, split),
        check_vma=False,
    )
```

```python
import functools

import jax
import jax.numpy as jnp
from jax import lax
from jax.experimental import pallas as pl
from jax.experimental.pallas import tpu as pltpu
from jax.sharding import PartitionSpec as P

GCAP = 15
SLOTS = 16
PAD = 8
LANES = 128
STEP = 512
SMALL = 4 * 2**20
FIELD = 32

root_two_pi = 0.7978845608028654
cubic_term = 0.044715

VM = pl.BlockSpec(memory_space=pltpu.VMEM)
SM = pl.BlockSpec(memory_space=pltpu.SMEM)
FAR = pl.BlockSpec(memory_space=pltpu.HBM)


def layout(rows, width):
    spare = PAD - rows
    pieces = -(-rows // spare)
    tail = 2 * width // (pieces + 1)
    return pieces, tail, 2 * width - tail


def gelu_both(v):
    t = jnp.tanh(root_two_pi * (v + cubic_term * v * v * v))
    value = 0.5 * v * (1.0 + t)
    slope = 0.5 * (1.0 + t) + 0.5 * v * (1.0 - t * t) * root_two_pi * (
        1.0 + 3.0 * cubic_term * v * v
    )
    return value, slope


def column(ref, choice, rows):
    row = lax.broadcasted_iota(jnp.int32, (rows, LANES), 0)
    out = jnp.zeros((rows, LANES), jnp.int32)
    for r in range(rows):
        out = jnp.where(row == r, ref[choice, r], out)
    return out


def pack_kernel(ids, slots, kept, tok, grad, gain, router, *outs):
    messages, (gates_ref, tok_out, grad_out, gain_out, router_out) = outs[:-5], outs[-5:]
    rows, width = tok.shape
    experts = router.shape[0]
    pieces, tail, head = layout(rows, width)
    me = lax.axis_index("expert")
    x = tok[...].astype(jnp.float32)
    g = grad[...].astype(jnp.float32)
    inverse = lax.rsqrt(jnp.mean(x * x, axis=1, keepdims=True) + 1e-06)
    normed = (x * inverse * gain[...]).astype(jnp.bfloat16)
    wide = normed.astype(jnp.float32)
    id0, id1 = column(ids, 0, rows), column(ids, 1, rows)
    pick0 = jnp.zeros((rows, LANES), jnp.float32)
    pick1 = jnp.zeros((rows, LANES), jnp.float32)
    for e in range(experts):
        logit = jnp.sum(wide * router[e : e + 1, :].astype(jnp.float32), axis=1, keepdims=True)
        pick0 = jnp.where(id0 == e, logit, pick0)
        pick1 = jnp.where(id1 == e, logit, pick1)
    gate0 = 1.0 / (1.0 + jnp.exp(pick1 - pick0))
    gate1 = 1.0 / (1.0 + jnp.exp(pick0 - pick1))
    gates_ref[...] = jnp.zeros_like(gates_ref)
    kept_for_later = (gate0, gate1, id0.astype(jnp.float32), id1.astype(jnp.float32), inverse)
    for i, entry in enumerate(kept_for_later):
        gates_ref[i * PAD : i * PAD + rows, :] = jnp.broadcast_to(entry, (rows, LANES))
    tok_out[...] = tok[...]
    grad_out[...] = grad[...]
    gain_out[...] = gain[...]
    router_out[...] = router[...]
    row = lax.broadcasted_iota(jnp.int32, (PAD, LANES), 0)
    field = lax.broadcasted_iota(jnp.int32, (PAD, LANES), 1) // FIELD
    for k, out in enumerate(messages):
        expert = me ^ k
        gate = jnp.where(id0 == expert, gate0, jnp.where(id1 == expert, gate1, 0.0))
        weighted = (gate[:, 0:1] * g).astype(jnp.bfloat16).astype(jnp.float32)
        low = []
        for first in range(0, rows, pieces):
            last = [weighted[r : r + 1, width - tail :] for r in range(first, min(first + pieces, rows))]
            last += [jnp.zeros((1, tail), jnp.float32)] * (pieces - len(last))
            low.append(jnp.concatenate(last, axis=1))
        high = jnp.concatenate([wide, weighted[:, : width - tail]], axis=1)
        out[:, :head] = jnp.concatenate([high] + low, axis=0).astype(jnp.bfloat16)
        table = jnp.full((PAD, LANES), -1, jnp.int32)
        for r in range(rows):
            hit0 = (ids[0, r] == expert) & (kept[0, r] == 1)
            hit1 = (ids[1, r] == expert) & (kept[1, r] == 1)
            slot = jnp.where(hit0, slots[0, r], jnp.where(hit1, slots[1, r], -1))
            here = (row == r) & (field == 0)
            there = (row == rows + r // pieces) & (field == 1 + r % pieces)
            table = jnp.where(here | there, slot, table)
        out[:, head:] = table.astype(jnp.float32).astype(jnp.bfloat16)


def bin_kernel(rows, width, done, *refs):
    del done
    messages, (bins, placed_ref) = refs[:-2], refs[-2:]
    pieces, tail, head = layout(rows, width)
    arrived = jnp.concatenate([m[...].astype(jnp.float32) for m in messages], axis=0)
    lane = lax.broadcasted_iota(jnp.int32, (arrived.shape[0], LANES), 1) % FIELD
    placed = jnp.where(arrived[:, head:] == lane.astype(jnp.float32), 1.0, 0.0)
    placed_ref[...] = placed
    onehot = placed.T.astype(jnp.bfloat16)
    packed = arrived[:, :head].astype(jnp.bfloat16)
    first = jnp.dot(onehot[:SLOTS], packed, preferred_element_type=jnp.float32)
    bins[0:SLOTS, :] = first[:, :width].astype(jnp.bfloat16)
    bins[SLOTS : 2 * SLOTS, : width - tail] = first[:, width:].astype(jnp.bfloat16)
    rest = 0.0
    for p in range(pieces):
        which = onehot[(p + 1) * FIELD : (p + 1) * FIELD + SLOTS]
        rest += jnp.dot(
            which, packed[:, p * tail : (p + 1) * tail], preferred_element_type=jnp.float32
        )
    bins[SLOTS : 2 * SLOTS, width - tail :] = rest.astype(jnp.bfloat16)


def later(gates, i, rows):
    return gates[i * PAD : i * PAD + rows, 0:1]


def prepare_kernel(start, gates, tok, gain, router, weight, out, done, *refs):
    scale, along, share, fixed, mean, sem = refs
    copy = pltpu.make_async_copy(weight.at[0, :, pl.ds(start, out.shape[1])], out, sem)
    copy.start()
    done[...] = gates[0:8, :]
    rows, width = tok.shape
    id0, id1, inverse = (later(gates, i, rows) for i in (2, 3, 4))
    x = tok[...].astype(jnp.float32)
    line = jnp.zeros((rows, width), jnp.float32)
    for e in range(router.shape[0]):
        sign = jnp.where(id0 == e, 1.0, 0.0) - jnp.where(id1 == e, 1.0, 0.0)
        line = line + sign * router[e : e + 1, :].astype(jnp.float32)
    scaled = gain[...] * inverse
    weighted = gain[...] * x
    scale[...] = scaled
    along[...] = x * inverse * inverse * inverse
    share[...] = weighted
    fixed[...] = line * scaled
    total = jnp.mean(line * weighted, axis=1, keepdims=True)
    mean[...] = jnp.broadcast_to(total, mean.shape)
    copy.wait()


def load_kernel(start, after, weight, out, done, sem):
    copy = pltpu.make_async_copy(weight.at[0, :, pl.ds(start, out.shape[1])], out, sem)
    copy.start()
    done[...] = after[0:8, :]
    copy.wait()


def expert_kernel(groups, *refs):
    bins, refs = refs[:groups], refs[groups:]
    _, _, down_hbm, up_a, up_b = refs[:5]
    outs, refs = refs[5 : 5 + groups], refs[5 + groups :]
    x, g, active, back_hidden, slope, down, sems = refs
    rows = groups * SLOTS
    width, early = up_a.shape
    hidden = early + up_b.shape[1]
    edges = [0, width // 3, width * 2 // 3, width]
    over = (((1,), (1,)), ((), ()))

    def fetch(i):
        at = pl.ds(edges[i], edges[i + 1] - edges[i])
        return pltpu.make_async_copy(down_hbm.at[0, at, :], down.at[at, :], sems.at[i])

    def columns(f):
        return (up_a, f) if f < early else (up_b, f - early)

    for i in range(len(edges) - 1):
        fetch(i).start()
    for j in range(groups):
        x[j * SLOTS : (j + 1) * SLOTS, :] = bins[j][0:SLOTS, :]
        g[j * SLOTS : (j + 1) * SLOTS, :] = bins[j][SLOTS : 2 * SLOTS, :]

    def deliver(part, at, side):
        for j, out in enumerate(outs):
            out[side * SLOTS : (side + 1) * SLOTS, at] = part[j * SLOTS : (j + 1) * SLOTS]

    taken = lax.axis_index("expert") >= 0

    @pl.when(taken)
    def _():
        for f in range(0, hidden, STEP):
            part, c = columns(f)
            v = jnp.dot(x[...], part[:, c : c + STEP], preferred_element_type=jnp.float32)
            value, rise = gelu_both(v[:rows])
            active[:, f : f + STEP] = value.astype(jnp.bfloat16)
            slope[:, f : f + STEP] = rise

    waiting = [(d, f) for d in range(0, width, STEP) for f in range(0, hidden, STEP)]
    share = -(-len(waiting) * 2 * STEP // (2 * width + hidden))

    def turn(count):
        for _ in range(min(count, len(waiting))):
            d, f = waiting.pop()
            part, c = columns(f)
            part[d : d + STEP, c : c + STEP] = part[d : d + STEP, c : c + STEP].T

    for i in range(len(edges) - 1):

        @pl.when(taken)
        def _(i=i):
            fetch(i).wait()
            for d in range(edges[i], edges[i + 1], STEP):
                turn(share)
                total = lax.dot_general(
                    down[d : d + STEP, :], active[...], over, preferred_element_type=jnp.float32
                )
                deliver(total.T.astype(jnp.bfloat16), slice(d, d + STEP), 0)

    @pl.when(taken)
    def _():
        for f in range(0, hidden, STEP):
            v = jnp.dot(g[...], down[:, f : f + STEP], preferred_element_type=jnp.float32)[:rows]
            back_hidden[0:rows, f : f + STEP] = (v * slope[:, f : f + STEP]).astype(jnp.bfloat16)
            turn(-(-share // 2))
        turn(len(waiting))

    for d in range(0, width, STEP):
        total = 0.0
        for f in range(0, hidden, STEP):
            part, c = columns(f)
            total += jnp.dot(
                back_hidden[:, f : f + STEP],
                part[d : d + STEP, c : c + STEP],
                preferred_element_type=jnp.float32,
            )
        deliver(total.astype(jnp.bfloat16), slice(d, d + STEP), 1)


def join_kernel(done, rows, out):
    del done
    out[...] = rows[...]


def add_kernel(a, b, out):
    total = a[...].astype(jnp.float32) + b[...].astype(jnp.float32)
    out[...] = total.astype(jnp.bfloat16)


def reply_kernel(rows, n_parts, *refs):
    parts, placed, replies = refs[:n_parts], refs[n_parts], refs[n_parts + 1 :]
    width = parts[0].shape[1]
    pieces, tail, head = layout(rows, width)
    total = parts[0][...].astype(jnp.float32)
    for p in parts[1:]:
        total = total + p[...].astype(jnp.float32)
    total = total.astype(jnp.bfloat16)
    both = jnp.concatenate([total[:SLOTS], total[SLOTS:]], axis=1)
    onehot = placed[...].astype(jnp.bfloat16)
    for p in range(pieces):
        at = slice(p * tail, (p + 1) * tail)
        which = onehot[:, (p + 1) * FIELD : (p + 1) * FIELD + SLOTS]
        spread = jnp.dot(onehot[:, :SLOTS], both[:, at], preferred_element_type=jnp.float32)
        spread += jnp.dot(which, both[:, head:], preferred_element_type=jnp.float32)
        for k, out in enumerate(replies):
            out[:, at] = spread[k * PAD : (k + 1) * PAD].astype(jnp.bfloat16)


def finish_kernel(grad, gates, scale, along, share, fixed, fixed_mean, *refs):
    replies, (mixed, grad_tokens) = refs[:-2], refs[-2:]
    rows, width = grad.shape
    pieces, tail, head = layout(rows, width)
    me = lax.axis_index("expert")
    gate0, gate1, id0, id1 = (later(gates, i, rows) for i in range(4))
    chosen0 = jnp.zeros((rows, width), jnp.float32)
    chosen1 = jnp.zeros((rows, width), jnp.float32)
    back = jnp.zeros((PAD, head), jnp.float32)
    for k, reply in enumerate(replies):
        expert = (me ^ k).astype(jnp.float32)
        answer = reply[...].astype(jnp.float32)
        chosen0 = jnp.where(id0 == expert, answer[:rows, :width], chosen0)
        chosen1 = jnp.where(id1 == expert, answer[:rows, :width], chosen1)
        back = back + answer
    rest = []
    for r in range(rows):
        p = r % pieces
        rest.append(back[rows + r // pieces : rows + r // pieces + 1, p * tail : (p + 1) * tail])
    back = jnp.concatenate([back[:rows, width:], jnp.concatenate(rest, axis=0)], axis=1)
    mixed[...] = (gate0 * chosen0 + gate1 * chosen1).astype(jnp.bfloat16)
    g = grad[...].astype(jnp.float32)
    spread = gate0 * gate1 * jnp.sum(g * (chosen0 - chosen1), axis=1, keepdims=True)
    mean = jnp.mean(back * share[...], axis=1, keepdims=True) + spread * fixed_mean[:, 0:1]
    grad_tokens[...] = (
        back * scale[...] + spread * fixed[...] - along[...] * mean
    ).astype(jnp.bfloat16)


def near(array):
    return pltpu.with_memory_space_constraint(array, pltpu.VMEM)


def far(array):
    return pltpu.with_memory_space_constraint(array, pltpu.HBM)


def call(body, out_shape, in_specs, args, limit=SMALL):
    return pl.pallas_call(
        body,
        out_shape=out_shape,
        in_specs=in_specs,
        out_specs=[VM] * len(out_shape),
        compiler_params=pltpu.CompilerParams(vmem_limit_bytes=limit),
    )(*args)


def shards(
    tokens, norm_gain, router, up_weight, down_weight, expert_ids, bin_slots, kept_mask, grad_out
):
    rows, width = tokens.shape
    hidden = up_weight.shape[2]
    experts = lax.axis_size("expert")
    groups = lax.axis_size("tensor")
    bf16, f32 = jnp.bfloat16, jnp.float32
    pieces, tail, head = layout(rows, width)

    def swap(array, axis, mask):
        n = lax.axis_size(axis)
        return lax.ppermute(array, axis, [(i, i ^ mask) for i in range(n)])

    ids, slots, kept = expert_ids.T, bin_slots.T, kept_mask.T
    gain, lines = norm_gain.reshape(1, width), router.T

    *messages, gates, tokens, grad_out, gain, lines = call(
        pack_kernel,
        [pltpu.VMEM((PAD, head + LANES), bf16)] * experts
        + [pltpu.VMEM((5 * PAD, LANES), f32)]
        + [pltpu.VMEM(a.shape, a.dtype) for a in (tokens, grad_out, gain, lines)],
        [SM] * 3 + [VM] * 4,
        (ids, slots, kept, tokens, grad_out, gain, lines),
        limit=None,
    )
    arrived = [messages[0]] + [swap(messages[k], "expert", k) for k in range(1, experts)]

    def load(body, start, stop, given, more):
        return pl.pallas_call(
            functools.partial(body, start),
            out_shape=[pltpu.VMEM((width, stop - start), bf16), pltpu.VMEM((8, LANES), f32)]
            + more,
            in_specs=[VM] * len(given) + [FAR],
            out_specs=[VM] * (2 + len(more)),
            scratch_shapes=[pltpu.SemaphoreType.DMA],
            compiler_params=pltpu.CompilerParams(vmem_limit_bytes=2**20),
            cost_estimate=pl.CostEstimate(
                flops=0, bytes_accessed=width * (stop - start) * 4, transcendentals=0
            ),
        )(*[near(a) for a in given], far(up_weight))

    early = max(STEP, hidden * 5 // 8 // STEP * STEP)
    up_a, done, *factors = load(
        prepare_kernel,
        0,
        early,
        (gates, tokens, gain, lines),
        [pltpu.VMEM((rows, width), f32)] * 4 + [pltpu.VMEM((rows, LANES), f32)],
    )

    own, placed = call(
        functools.partial(bin_kernel, rows, width),
        [pltpu.VMEM((2 * SLOTS, width), bf16), pltpu.VMEM((experts * PAD, LANES), f32)],
        [VM] * (1 + experts),
        [near(a) for a in (done, *arrived)],
    )
    up_b, done = load(load_kernel, early, hidden, (placed,), [])

    mask = groups // 2
    far_rows = call(
        join_kernel,
        [pltpu.VMEM((2 * SLOTS, width), bf16)],
        [VM] * 2,
        [near(a) for a in (done, swap(own, "tensor", mask))],
    )[0]
    bins = {0: own, mask: far_rows}
    mask //= 2
    while mask:
        bins.update({j | mask: swap(b, "tensor", mask) for j, b in bins.items()})
        mask //= 2

    tall = max(groups * SLOTS, 128)
    short = groups * SLOTS
    _, _, *sums = pl.pallas_call(
        functools.partial(expert_kernel, groups),
        out_shape=[pltpu.VMEM(up_a.shape, bf16), pltpu.VMEM(up_b.shape, bf16)]
        + [pltpu.VMEM((2 * SLOTS, width), bf16)] * groups,
        input_output_aliases={groups: 0, groups + 1: 1},
        in_specs=[VM] * (groups + 2) + [FAR],
        out_specs=[VM] * (groups + 2),
        scratch_shapes=[
            pltpu.VMEM((tall, width), bf16),
            pltpu.VMEM((tall, width), bf16),
            pltpu.VMEM((short, hidden), bf16),
            pltpu.VMEM((tall, hidden), bf16),
            pltpu.VMEM((short, hidden), f32),
            pltpu.VMEM((width, hidden), bf16),
            pltpu.SemaphoreType.DMA((3,)),
        ],
        compiler_params=pltpu.CompilerParams(vmem_limit_bytes=32 * 2**20),
    )(*[near(bins[j]) for j in range(groups)], near(up_a), near(up_b), far(down_weight))

    piece = pltpu.VMEM((2 * SLOTS, width), bf16)
    firsts = [sums[0], swap(sums[1], "tensor", 1)]
    sums = {
        j: (sums[j].astype(f32) + swap(sums[j + 1], "tensor", 1).astype(f32)).astype(bf16)
        for j in range(2, groups, 2)
    }
    mask = 2
    while mask < groups:
        came = {j ^ mask: swap(a, "tensor", mask) for j, a in sums.items() if j & mask}
        sums = {j: a for j, a in sums.items() if not j & mask}
        for j, a in came.items():
            if j == 0:
                firsts.append(a)
            else:
                sums[j] = call(add_kernel, [piece], [VM] * 2, (near(sums[j]), near(a)))[0]
        mask *= 2

    replies = call(
        functools.partial(reply_kernel, rows, len(firsts)),
        [pltpu.VMEM((PAD, head), bf16)] * experts,
        [VM] * (len(firsts) + 1),
        [near(a) for a in (*firsts, placed)],
    )
    answers = [replies[0]] + [swap(replies[k], "expert", k) for k in range(1, experts)]

    result = jax.ShapeDtypeStruct((rows, width), bf16)
    mixed, grad_tokens = call(
        finish_kernel,
        [result, result],
        [VM] * (7 + experts),
        [near(a) for a in (grad_out, gates, *factors, *answers)],
    )
    return mixed, grad_tokens


def solution(mesh):
    split = P(("dp", "expert", "tensor"), None)
    weights = P("expert", None, "tensor")
    return jax.shard_map(
        shards,
        mesh=mesh,
        in_specs=(split, P(), P(), weights, weights, split, split, split, split),
        out_specs=(split, split),
        check_vma=False,
    )
```
